256 devices in a mesh: lat: 16 (over x, y), lon: 16 (over z, core).
Axes of the slice: x: 4, y: 4, z: 8, core: 2. Of those that a mesh axis runs over, the one named last changes fastest.
Arguments:
- features: bfloat16 [256, 1440, 256], P('lat', 'lon'), may hold values from -6 to 6
- cotangent: bfloat16 [256, 1440, 256], P('lat', 'lon'), may hold values from -6 to 6
- disco_basis: bfloat16 [3, 256, 3, 33], replicated, may hold values from -0.875 to 0.875
- support_width: int32 [256], replicated, may hold values from 1 to 16, as said below
- mix_weight: bfloat16 [3, 256, 256], replicated, may hold values from -0.21875 to 0.21875
- spectral_filter: float32 [2, 720, 256], replicated, may hold values from -6 to 6
Outputs:
- block_output: bfloat16 [256, 1440, 256], P('lat', 'lon')
- grad_input: bfloat16 [256, 1440, 256], P('lat', 'lon')
- grad_weight: float32 [3, 256, 256], replicated
- grad_filter: float32 [2, 720, 256], replicated
The draws below stay inside these ranges and needn't reach their ends.
Inputs may be any that keep to these rules, and one draw needn't show every extreme that they name: `support_width`: longitude half-width in cells of the DISCO support at each latitude row.
All inputs are finite; a program needn't handle non-finite values.
Results may differ from the reference program's by a relative error of at most 0.0076.
Values may be sent and summed in bfloat16 or wider, within the bound.
A program may use at most 128 MiB of HBM per device.

```python
import math
import jax
import jax.numpy as jnp
from jax import lax

C = 256
NLON = 1440
MODES = 720
K = 3
S_MAX = 16
NLAT = 256
N_LON = 16


def draw_support_width(key, part):
    key = jax.random.fold_in(key, 7)
    row_index = jnp.arange(NLAT, dtype=jnp.int32)
    distance = jnp.minimum(row_index, NLAT - 1 - row_index)
    polar_width = S_MAX - distance * 2 * S_MAX // NLAT
    scatter_width = jax.random.randint(key, (NLAT,), 1, S_MAX // 2 + 1, dtype=jnp.int32)
    return jnp.maximum(polar_width, scatter_width).astype(jnp.int32)


def block_scale(key, shape, split, least, top_value):
    def one(position, parts):
        steps = jax.random.uniform(jax.random.fold_in(jax.random.fold_in(key, 6), position), (parts,), jnp.float32, least / len(split), top_value / len(split))
        return jnp.repeat(jnp.exp(steps), shape[position] // parts).reshape((-1,) + (1,) * (len(shape) - position - 1))

    level = one(*split[0])
    for cut in split[1:]:
        level = level * one(*cut)
    return level


def centred(own_key, shape, width, bound, shards=(), kind=jnp.bfloat16):
    gain = block_scale(own_key, shape, shards, -0.22, 0.18) if shards else 1.0
    array = jax.random.normal(own_key, shape, jnp.float32) * width * gain
    return jnp.minimum(jnp.maximum(array, -bound), bound).astype(kind)


def setup_inputs(seed: int = 0) -> dict:
    seeds = jax.random.split(jax.random.key(seed), 7)
    return {
        "features": centred(seeds[0], (NLAT, NLON, C), 1.0, 6.0, ((0, 16), (1, 16))),
        "cotangent": centred(seeds[1], (NLAT, NLON, C), 1.0, 6.0, ((0, 16), (1, 16))),
        "disco_basis": centred(seeds[2], (K, NLAT, 3, 2 * S_MAX + 1), 0.15, 0.875),
        "support_width": draw_support_width(jax.random.fold_in(seeds[6], 71), 0),
        "mix_weight": centred(seeds[4], (K, C, C), (K * C) ** -0.5, 0.21875),
        "spectral_filter": centred(seeds[5], (2, MODES, C), 1.0, 6.0, (), jnp.float32),
    }


def masked_basis(disco_basis, support_width):
    spread = disco_basis.shape[3] // 2
    offsets = jnp.abs(jnp.arange(2 * spread + 1, dtype=jnp.int32) - spread)
    retained = offsets[None, :] <= support_width[:, None]
    return jnp.where(retained[None, :, None, :], disco_basis, jnp.zeros_like(disco_basis))


def band_tables(spread, columns):
    outer = jnp.arange(columns + 2 * spread, dtype=jnp.int32)
    inner = jnp.arange(columns, dtype=jnp.int32)
    taps = jnp.arange(2 * spread + 1, dtype=jnp.int32)
    forward_hot = (outer[:, None, None] - inner[None, :, None] == taps[None, None, :]).astype(jnp.float32)
    backward_hot = (inner[None, :, None] - outer[:, None, None] + 2 * spread == taps[None, None, :]).astype(jnp.float32)
    return forward_hot, backward_hot


def dft_tables(longitudes, wavenumbers):
    cell_index = jnp.arange(longitudes, dtype=jnp.int32)
    wave_index = jnp.arange(wavenumbers, dtype=jnp.int32)
    phase_index = (wave_index[:, None] * cell_index[None, :]) % longitudes
    angles = phase_index.astype(jnp.float32) * (2.0 * math.pi / longitudes)
    cosine_wave = jnp.cos(angles)
    sine_wave = jnp.sin(angles)
    forward_table = jnp.concatenate([cosine_wave, -sine_wave], axis=0).astype(jnp.bfloat16)
    factor = jnp.where(wave_index == 0, 1.0, 2.0).astype(jnp.float32) / longitudes
    inverse_table = jnp.concatenate([cosine_wave * factor[:, None], -sine_wave * factor[:, None]], axis=0).T.astype(jnp.bfloat16)
    return forward_table, inverse_table


def silu_slope(values):
    logistic = jax.nn.sigmoid(values)
    return logistic * (1.0 + values * (1.0 - logistic))


def wrap_pad(field, spread):
    row_padded = jnp.pad(field, ((1, 1), (0, 0), (0, 0)))
    return jnp.concatenate([row_padded[:, -spread:], row_padded, row_padded[:, :spread]], axis=1)


def join_blocks(blocks):
    moved = jnp.transpose(blocks, (1, 0, 2, 3))
    return moved.reshape(moved.shape[0], moved.shape[1] * moved.shape[2], moved.shape[3])


def disco_apply(forward_band, input_slab):
    row_count = input_slab.shape[0] - 2
    running = jnp.zeros((forward_band.shape[0], row_count, forward_band.shape[4], input_slab.shape[2]), jnp.float32)
    for offset in range(3):
        running = running + jnp.einsum('kiaj,iac->kijc', forward_band[:, :, offset].astype(jnp.float32), input_slab[offset:offset + row_count].astype(jnp.float32))
    return running.astype(jnp.bfloat16)


def disco_adjoint(backward_band, kernel_grad):
    row_count = kernel_grad.shape[1] - 2
    running = jnp.zeros((row_count, backward_band.shape[4], kernel_grad.shape[3]), jnp.float32)
    for offset in range(3):
        lower = 2 - offset
        running = running + jnp.einsum('kiqb,kiqc->ibc', backward_band[:, lower:lower + row_count, offset].astype(jnp.float32), kernel_grad[:, lower:lower + row_count].astype(jnp.float32))
    return running


def reference(features, cotangent, disco_basis, support_width, mix_weight, spectral_filter):
    columns = NLON // N_LON
    spread = S_MAX
    effective = masked_basis(disco_basis, support_width)
    padded_basis = jnp.pad(effective, ((0, 0), (1, 1), (0, 0), (0, 0)))
    forward_hot, backward_hot = band_tables(spread, columns)
    forward_band = jnp.einsum('kirs,ajs->kiraj', effective.astype(jnp.float32), forward_hot).astype(jnp.bfloat16)
    backward_band = jnp.einsum('kirs,qbs->kirqb', padded_basis.astype(jnp.float32), backward_hot).astype(jnp.bfloat16)
    forward_table, inverse_table = dft_tables(NLON, MODES)
    spectrum = jnp.einsum('mn,inc->imc', forward_table.astype(jnp.float32), features.astype(jnp.float32))
    real_gain = spectral_filter[0]
    imag_gain = spectral_filter[1]
    real_part = spectrum[:, :MODES]
    imag_part = spectrum[:, MODES:]
    filtered = jnp.concatenate([real_gain * real_part - imag_gain * imag_part, real_gain * imag_part + imag_gain * real_part], axis=1).astype(jnp.bfloat16)
    spectral = jnp.einsum('nm,imc->inc', inverse_table.astype(jnp.float32), filtered.astype(jnp.float32)).astype(jnp.bfloat16)
    starts = jnp.arange(N_LON, dtype=jnp.int32) * columns
    padded_input = wrap_pad(features, spread)

    def forward_block(block_start):
        input_slab = lax.dynamic_slice_in_dim(padded_input, block_start, columns + 2 * spread, 1)
        kernel_out = disco_apply(forward_band, input_slab)
        disco_out = jnp.einsum('kijc,kcd->ijd', kernel_out.astype(jnp.float32), mix_weight.astype(jnp.float32))
        own_input = lax.dynamic_slice_in_dim(features, block_start, columns, 1)
        own_spectral = lax.dynamic_slice_in_dim(spectral, block_start, columns, 1)
        own_cotangent = lax.dynamic_slice_in_dim(cotangent, block_start, columns, 1)
        preact = disco_out + own_spectral.astype(jnp.float32)
        output = (own_input.astype(jnp.float32) + jax.nn.silu(preact)).astype(jnp.bfloat16)
        slope_grad = (own_cotangent.astype(jnp.float32) * silu_slope(preact)).astype(jnp.bfloat16)
        mix_part = jnp.einsum('kijc,ijd->kcd', kernel_out.astype(jnp.float32), slope_grad.astype(jnp.float32))
        return output, slope_grad, mix_part

    outputs, slopes, mix_parts = lax.map(forward_block, starts)
    block_output = join_blocks(outputs)
    pre_grad = join_blocks(slopes)
    grad_weight = jnp.sum(mix_parts, axis=0)
    cot_modes = jnp.einsum('nm,inc->imc', inverse_table.astype(jnp.float32), pre_grad.astype(jnp.float32))
    real_cot = cot_modes[:, :MODES]
    imag_cot = cot_modes[:, MODES:]
    grad_filter = jnp.stack([jnp.sum(real_cot * real_part + imag_cot * imag_part, axis=0), jnp.sum(imag_cot * real_part - real_cot * imag_part, axis=0)])
    back_modes = jnp.concatenate([real_gain * real_cot + imag_gain * imag_cot, real_gain * imag_cot - imag_gain * real_cot], axis=1).astype(jnp.bfloat16)
    spectral_grad = jnp.einsum('mn,imc->inc', forward_table.astype(jnp.float32), back_modes.astype(jnp.float32)).astype(jnp.bfloat16)
    padded_grad = wrap_pad(pre_grad, spread)

    def backward_block(block_start):
        grad_slab = lax.dynamic_slice_in_dim(padded_grad, block_start, columns + 2 * spread, 1)
        kernel_grad = jnp.einsum('pqd,kcd->kpqc', grad_slab.astype(jnp.float32), mix_weight.astype(jnp.float32)).astype(jnp.bfloat16)
        return disco_adjoint(backward_band, kernel_grad)

    conv_grad = join_blocks(lax.map(backward_block, starts))
    grad_input = (cotangent.astype(jnp.float32) + conv_grad + spectral_grad.astype(jnp.float32)).astype(jnp.bfloat16)
    return block_output, grad_input, grad_weight, grad_filter
```

```python
import math

import jax
import jax.numpy as jnp
import ml_dtypes
import numpy as np
from jax import lax
from jax.sharding import PartitionSpec as P


def extended(value, sides, width, wrap):
    for axis, dim in sides:
        size, length = (lax.axis_size(axis), value.shape[dim])
        up = [(i, (i + 1) % size) for i in range(size if wrap else size - 1)]
        down = [(j, i) for i, j in up]
        last = lax.slice_in_dim(value, length - width, length, axis=dim)
        initial = lax.slice_in_dim(value, 0, width, axis=dim)
        before = lax.ppermute(last, axis, up)
        after = lax.ppermute(initial, axis, down)
        value = jnp.concatenate([before, value, after], axis=dim)
    return value


def masked_basis(disco_basis, support_width):
    spread = disco_basis.shape[3] // 2
    offsets = jnp.abs(jnp.arange(2 * spread + 1, dtype=jnp.int32) - spread)
    retained = offsets[None, :] <= support_width[:, None]
    return jnp.where(retained[None, :, None, :], disco_basis, jnp.zeros_like(disco_basis))


def band_tables(spread, columns):
    outer = jnp.arange(columns + 2 * spread, dtype=jnp.int32)
    inner = jnp.arange(columns, dtype=jnp.int32)
    taps = jnp.arange(2 * spread + 1, dtype=jnp.int32)
    forward_hot = (outer[:, None, None] - inner[None, :, None] == taps[None, None, :]).astype(
        jnp.float32
    )
    backward_hot = (
        inner[None, :, None] - outer[:, None, None] + 2 * spread == taps[None, None, :]
    ).astype(jnp.float32)
    return (forward_hot, backward_hot)


def dft_tables(longitudes, wavenumbers):
    cell_index = np.arange(longitudes, dtype=np.int64)
    wave_index = np.arange(wavenumbers, dtype=np.int64)
    phase_index = wave_index[:, None] * cell_index[None, :] % longitudes
    angles = phase_index.astype(np.float32) * np.float32(2.0 * math.pi / longitudes)
    cosine_wave = np.cos(angles)
    sine_wave = np.sin(angles)
    forward_table = np.concatenate([cosine_wave, -sine_wave], axis=0).astype(ml_dtypes.bfloat16)
    factor = np.where(wave_index == 0, 1.0, 2.0).astype(np.float32) / np.float32(longitudes)
    inverse_table = np.concatenate(
        [cosine_wave * factor[:, None], -sine_wave * factor[:, None]], axis=0
    ).T.astype(ml_dtypes.bfloat16)
    return (jnp.asarray(forward_table), jnp.asarray(np.ascontiguousarray(inverse_table)))


def total(value):
    flat = value.reshape(-1, value.shape[-1])
    part = lax.psum_scatter(flat, "lat", scatter_dimension=0, tiled=True)
    part = lax.psum(part, "lon")
    return lax.all_gather(part, "lat", axis=0, tiled=True).reshape(value.shape)


def silu_slope(values):
    logistic = jax.nn.sigmoid(values)
    return logistic * (1.0 + values * (1.0 - logistic))


def disco_apply(forward_band, input_slab):
    row_count = input_slab.shape[0] - 2
    running = jnp.zeros(
        (forward_band.shape[0], row_count, forward_band.shape[4], input_slab.shape[2]), jnp.float32
    )
    for offset in range(3):
        running = running + jnp.einsum(
            "kiaj,iac->kijc",
            forward_band[:, :, offset],
            input_slab[offset : offset + row_count],
            preferred_element_type=jnp.float32,
        )
    return running.astype(jnp.bfloat16)


def disco_adjoint(backward_band, kernel_grad):
    row_count = kernel_grad.shape[1] - 2
    running = jnp.zeros((row_count, backward_band.shape[4], kernel_grad.shape[3]), jnp.float32)
    for offset in range(3):
        lower = 2 - offset
        running = running + jnp.einsum(
            "kiqb,kiqc->ibc",
            backward_band[:, lower : lower + row_count, offset],
            kernel_grad[:, lower : lower + row_count],
            preferred_element_type=jnp.float32,
        )
    return running


def to_modes(forward_table, field, gain_table):
    spectrum = jnp.einsum("mn,inc->imc", forward_table, field, preferred_element_type=jnp.float32)
    wavenumbers = gain_table.shape[1]
    real_part = spectrum[:, :wavenumbers]
    imag_part = spectrum[:, wavenumbers:]
    real_gain = gain_table[0]
    imag_gain = gain_table[1]
    filtered = jnp.concatenate(
        [
            real_gain * real_part - imag_gain * imag_part,
            real_gain * imag_part + imag_gain * real_part,
        ],
        axis=1,
    ).astype(jnp.bfloat16)
    return (spectrum, filtered)


def from_modes(inverse_table, filtered):
    return jnp.einsum(
        "nm,imc->inc", inverse_table, filtered, preferred_element_type=jnp.float32
    ).astype(jnp.bfloat16)


def adjoint_modes(forward_table, inverse_table, cot_field, spectrum, gain_table):
    wavenumbers = gain_table.shape[1]
    cot_modes = jnp.einsum(
        "nm,inc->imc", inverse_table, cot_field, preferred_element_type=jnp.float32
    )
    real_cot = cot_modes[:, :wavenumbers]
    imag_cot = cot_modes[:, wavenumbers:]
    real_part = spectrum[:, :wavenumbers]
    imag_part = spectrum[:, wavenumbers:]
    real_gain = gain_table[0]
    imag_gain = gain_table[1]
    gradient = jnp.stack(
        [
            jnp.sum(real_cot * real_part + imag_cot * imag_part, axis=0),
            jnp.sum(imag_cot * real_part - real_cot * imag_part, axis=0),
        ]
    )
    back_modes = jnp.concatenate(
        [real_gain * real_cot + imag_gain * imag_cot, real_gain * imag_cot - imag_gain * real_cot],
        axis=1,
    ).astype(jnp.bfloat16)
    spectral_grad = jnp.einsum(
        "mn,imc->inc", forward_table, back_modes, preferred_element_type=jnp.float32
    ).astype(jnp.bfloat16)
    return (gradient, spectral_grad)


def on_device(features, cotangent, disco_basis, support_width, mix_weight, spectral_filter):
    row_count, columns, channels = features.shape
    spread = disco_basis.shape[3] // 2
    wavenumbers = spectral_filter.shape[1]
    lon_devices = lax.axis_size("lon")
    longitudes = columns * lon_devices
    first_row = lax.axis_index("lat") * row_count
    effective = masked_basis(disco_basis, support_width)
    padded_basis = jnp.pad(effective, ((0, 0), (1, 1), (0, 0), (0, 0)))
    local_basis = lax.dynamic_slice_in_dim(padded_basis, first_row, row_count + 2, 1)
    forward_hot, backward_hot = band_tables(spread, columns)
    forward_band = jnp.einsum(
        "kirs,ajs->kiraj", local_basis[:, 1 : row_count + 1].astype(jnp.float32), forward_hot
    ).astype(jnp.bfloat16)
    backward_band = jnp.einsum(
        "kirs,qbs->kirqb", local_basis.astype(jnp.float32), backward_hot
    ).astype(jnp.bfloat16)
    forward_table, inverse_table = dft_tables(longitudes, wavenumbers)
    lat_padded = extended(features, (("lat", 0),), 1, False)
    input_slab = extended(lat_padded, (("lon", 1),), spread, True)
    kernel_out = disco_apply(forward_band, input_slab)
    disco_out = jnp.einsum(
        "kijc,kcd->ijd", kernel_out, mix_weight, preferred_element_type=jnp.float32
    )
    gathered = lax.all_to_all(features, "lon", split_axis=0, concat_axis=1, tiled=True)
    spectrum, filtered = to_modes(forward_table, gathered, spectral_filter)
    spectral = lax.all_to_all(
        from_modes(inverse_table, filtered), "lon", split_axis=1, concat_axis=0, tiled=True
    )
    preact = disco_out + spectral.astype(jnp.float32)
    block_output = (features.astype(jnp.float32) + jax.nn.silu(preact)).astype(jnp.bfloat16)
    pre_grad = (cotangent.astype(jnp.float32) * silu_slope(preact)).astype(jnp.bfloat16)
    mix_part = jnp.einsum("kijc,ijd->kcd", kernel_out, pre_grad, preferred_element_type=jnp.float32)
    cot_field = lax.all_to_all(pre_grad, "lon", split_axis=0, concat_axis=1, tiled=True)
    filter_part, owner_grad = adjoint_modes(
        forward_table, inverse_table, cot_field, spectrum, spectral_filter
    )
    spectral_grad = lax.all_to_all(owner_grad, "lon", split_axis=1, concat_axis=0, tiled=True)
    grad_weight, grad_filter = (total(mix_part), total(filter_part))
    products = jnp.einsum(
        "ijd,kcd->kijc", pre_grad, mix_weight, preferred_element_type=jnp.float32
    ).astype(jnp.bfloat16)
    product_rim = extended(products, (("lat", 1),), 1, False)
    kernel_grad = extended(product_rim, (("lon", 2),), spread, True)
    conv_grad = disco_adjoint(backward_band, kernel_grad)
    grad_input = (
        cotangent.astype(jnp.float32) + conv_grad + spectral_grad.astype(jnp.float32)
    ).astype(jnp.bfloat16)
    return (block_output, grad_input, grad_weight, grad_filter)


def solution(mesh):
    return jax.shard_map(
        on_device,
        mesh=mesh,
        in_specs=(P("lat", "lon", None), P("lat", "lon", None), P(), P(), P(), P()),
        out_specs=(P("lat", "lon", None), P("lat", "lon", None), P(), P()),
        check_vma=False,
    )
```

```python
import functools
import math

import jax
import jax.numpy as jnp
import ml_dtypes
import numpy as np
from jax import lax
from jax.experimental import pallas as pl
from jax.experimental.pallas import tpu as pltpu
from jax.sharding import PartitionSpec as P

MESH = pl.DeviceIdType.MESH
F32 = jnp.float32
BF16 = jnp.bfloat16

ROWS = 16
COLS = 90
PAD = 96
WAVES = 720
WAVES_PAD = 768
SPREAD = 16
LANES = 128
CHANNELS = 256
WIDE = 128
TILE = 384


def masked_basis(disco_basis, support_width):
    spread = disco_basis.shape[3] // 2
    offsets = jnp.abs(jnp.arange(2 * spread + 1, dtype=jnp.int32) - spread)
    retained = offsets[None, :] <= support_width[:, None]
    return jnp.where(retained[None, :, None, :], disco_basis, jnp.zeros_like(disco_basis))


def dft_tables():
    longitudes = ROWS * COLS
    cell_index = np.arange(longitudes, dtype=np.int64)
    wave_index = np.arange(WAVES, dtype=np.int64)
    phase_index = wave_index[:, None] * cell_index[None, :] % longitudes
    angles = phase_index.astype(np.float32) * np.float32(2.0 * math.pi / longitudes)
    cosine_wave = np.cos(angles)
    sine_wave = np.sin(angles)
    factor = np.where(wave_index == 0, 1.0, 2.0).astype(np.float32) / np.float32(longitudes)

    def padded(real, imag):
        table = np.zeros((2, WAVES_PAD, ROWS, PAD), np.float32)
        table[0, :WAVES, :, :COLS] = real.reshape(WAVES, ROWS, COLS)
        table[1, :WAVES, :, :COLS] = imag.reshape(WAVES, ROWS, COLS)
        return table.reshape(2 * WAVES_PAD, ROWS * PAD).astype(ml_dtypes.bfloat16)

    forward = padded(cosine_wave, -sine_wave)
    inverse_t = padded(cosine_wave * factor[:, None], -sine_wave * factor[:, None])
    return (
        forward,
        np.ascontiguousarray(inverse_t.T),
        inverse_t,
        np.ascontiguousarray(forward.T),
    )


def kernel(
    x_ref, ct_ref, vf_ref, vb_ref, mix_ref, sf_ref, t0_ref, t1_ref, t2_ref, t3_ref,
    out_ref, gin_ref, gw_ref, gf_ref,
    tables, cts, slab, pslab, tail, ptail, xs, g1, ys, s1, ps, g2, zs, s2,
    resp, dense, spectrum, cotspec, modes, band,
    ws, wr, w2s, w2r, w3, wfin, fs, fr, f2s, f2r, f3, ffin,
    table_sem, a_send, a_recv, halo_send, halo_recv, ar_send, ar_recv,
):
    me = lax.axis_index("lon")
    lat = lax.axis_index("lat")
    right = lax.rem(me + 1, ROWS)
    left = lax.rem(me + ROWS - 1, ROWS)

    table_copies = [
        pltpu.make_async_copy(ref, tables.at[i], table_sem.at[i])
        for i, ref in enumerate((t0_ref, t1_ref, t2_ref, t3_ref))
    ]
    for copy in table_copies:
        copy.start()

    barrier = pltpu.get_barrier_semaphore()

    def greet(step, carry):
        pl.semaphore_signal(
            barrier, inc=1, device_id={"lon": lax.rem(me + step, ROWS)}, device_id_type=MESH
        )
        pl.semaphore_signal(
            barrier, inc=1, device_id={"lat": lax.rem(lat + step, ROWS)}, device_id_type=MESH
        )
        return carry

    lax.fori_loop(1, ROWS, greet, 0)

    def pack(i, carry):
        slab[i + 1, 80:PAD, :] = jnp.zeros((PAD - 80, CHANNELS), BF16)
        slab[i + 1, 0:COLS, :] = x_ref[i]
        cts[i, 80:PAD, :] = jnp.zeros((PAD - 80, CHANNELS), BF16)
        cts[i, 0:COLS, :] = ct_ref[i]
        for h in range(2):
            xs[h, i] = slab[i + 1, 0:PAD, h * LANES : (h + 1) * LANES]
        return carry

    lax.fori_loop(0, ROWS, pack, 0)
    pl.semaphore_wait(barrier, 2 * (ROWS - 1))

    def offset(step):
        return 8 + (1 - 2 * lax.rem(step, 2)) * lax.div(step + 1, 2)

    def spread_start(source, target, h, phase):
        def body(step, carry):
            peer = lax.rem(me + offset(step), ROWS)
            pltpu.make_async_remote_copy(
                src_ref=source.at[h, peer],
                dst_ref=target.at[h, me],
                send_sem=a_send.at[phase, h],
                recv_sem=a_recv.at[phase, h],
                device_id={"lon": peer},
                device_id_type=MESH,
            ).start()
            return carry

        lax.fori_loop(0, ROWS - 1, body, 0)

    def own_piece(source, target, h):
        target[h, me] = source[h, me]

    def wait_bytes(ref, sem):
        pltpu.make_async_copy(ref, ref, sem).wait()

    def spread_wait(target, h, phase):
        wait_bytes(target.at[h, pl.ds(0, ROWS - 1)], a_recv.at[phase, h])

    def halo_copy(src, dst, index, device):
        return pltpu.make_async_remote_copy(
            src_ref=src,
            dst_ref=dst,
            send_sem=halo_send.at[index],
            recv_sem=halo_recv.at[index],
            device_id=device,
            device_id_type=MESH,
        )

    def lat_halo(buf, base):
        up = halo_copy(
            buf.at[1, pl.ds(0, PAD)], buf.at[17, pl.ds(0, PAD)], base, {"lat": lax.max(lat - 1, 0)}
        )
        down = halo_copy(
            buf.at[16, pl.ds(0, PAD)],
            buf.at[0, pl.ds(0, PAD)],
            base + 1,
            {"lat": lax.min(lat + 1, ROWS - 1)},
        )
        return up, down

    def lon_halo(buf, end, base):
        pairs = []
        for n, rows in enumerate((pl.ds(1, ROWS), pl.ds(0, 1), pl.ds(17, 1))):
            pairs.append(
                (
                    halo_copy(
                        buf.at[rows, pl.ds(0, SPREAD)],
                        buf.at[rows, pl.ds(PAD, SPREAD)],
                        base + 2 + 2 * n,
                        {"lon": left},
                    ),
                    halo_copy(
                        end.at[rows],
                        buf.at[rows, pl.ds(PAD + SPREAD, SPREAD)],
                        base + 3 + 2 * n,
                        {"lon": right},
                    ),
                )
            )
        return pairs

    def tail_row(buf, end, i):
        moved = pltpu.roll(buf[i, 0:PAD, :].astype(F32), PAD - COLS, 0)
        end[i] = moved[PAD - SPREAD : PAD].astype(BF16)

    def halo_begin(buf, end, base):
        up, down = lat_halo(buf, base)

        @pl.when(lat > 0)
        def _():
            up.start()

        @pl.when(lat < ROWS - 1)
        def _():
            down.start()

        def body(i, carry):
            tail_row(buf, end, i + 1)
            return carry

        lax.fori_loop(0, ROWS, body, 0)
        for copy in lon_halo(buf, end, base)[0]:
            copy.start()

    def halo_middle(buf, end, base):
        up, down = lat_halo(buf, base)

        @pl.when(lat > 0)
        def _():
            down.wait_recv()

        @pl.when(lat == 0)
        def _():
            buf[0, 0:PAD, :] = jnp.zeros((PAD, CHANNELS), BF16)

        @pl.when(lat < ROWS - 1)
        def _():
            up.wait_recv()

        @pl.when(lat == ROWS - 1)
        def _():
            buf[17, 0:PAD, :] = jnp.zeros((PAD, CHANNELS), BF16)

        tail_row(buf, end, 0)
        tail_row(buf, end, 17)
        for pair in lon_halo(buf, end, base)[1:]:
            for copy in pair:
                copy.start()

    def halo_wait(buf, end, base):
        for pair in lon_halo(buf, end, base):
            for copy in pair:
                copy.wait_recv()

    def halo_end(buf, end, base):
        up, down = lat_halo(buf, base)

        @pl.when(lat > 0)
        def _():
            up.wait_send()

        @pl.when(lat < ROWS - 1)
        def _():
            down.wait_send()

        for pair in lon_halo(buf, end, base):
            for copy in pair:
                copy.wait_send()

    lane = lax.broadcasted_iota(jnp.int32, (PAD, WIDE), 1)
    row = lax.broadcasted_iota(jnp.int32, (PAD, WIDE), 0)
    direct = (row < COLS) & ((lane < COLS) | (lane >= PAD + SPREAD))
    shifted = (row < COLS) & (lane >= PAD) & (lane < PAD + SPREAD)

    def apply_band(vec_ref, buf):
        def body(i, carry):
            for k in range(3):
                for r in range(3):
                    vec = jnp.broadcast_to(vec_ref[i, 3 * k + r : 3 * k + r + 1, :], (PAD, WIDE))
                    near = pltpu.roll(vec, 0, 1, stride=1, stride_axis=0)
                    far = pltpu.roll(vec, PAD - COLS, 1, stride=1, stride_axis=0)
                    part = jnp.where(direct, near, jnp.where(shifted, far, 0.0))
                    band[k * PAD : (k + 1) * PAD, r * WIDE : (r + 1) * WIDE] = part.astype(BF16)
            around = buf[pl.ds(i, 3)].reshape(3 * WIDE, CHANNELS)
            value = jnp.dot(band[...], around, preferred_element_type=F32).astype(BF16)
            for k in range(3):
                resp[k, i] = value[k * PAD : (k + 1) * PAD]
            return carry

        lax.fori_loop(0, ROWS, body, 0)

    def mix(transposed):
        def body(n, carry):
            total = jnp.zeros((TILE, CHANNELS), F32)
            for k in range(3):
                part = resp[k, pl.ds(4 * n, 4)].reshape(TILE, CHANNELS)
                total = total + lax.dot_general(
                    part,
                    mix_ref[k],
                    (((1,), (1 if transposed else 0,)), ((), ())),
                    preferred_element_type=F32,
                )
            dense[pl.ds(4 * n, 4)] = total.reshape(4, PAD, CHANNELS)
            return carry

        lax.fori_loop(0, 4, body, 0)

    def to_spectrum(table, field, h, target):
        def body(n, carry):
            rows = pl.ds(pl.multiple_of(n * TILE, TILE), TILE)
            target[rows, :] = jnp.dot(
                tables[table, rows, :],
                field[h].reshape(ROWS * PAD, LANES),
                preferred_element_type=F32,
            )
            return carry

        lax.fori_loop(0, 4, body, 0)

    def to_field(table, field, h):
        def body(n, carry):
            rows = pl.ds(pl.multiple_of(n * TILE, TILE), TILE)
            value = jnp.dot(tables[table, rows, :], modes[...], preferred_element_type=F32)
            field[h, pl.ds(4 * n, 4)] = value.astype(BF16).reshape(4, PAD, LANES)
            return carry

        lax.fori_loop(0, 4, body, 0)

    for h in range(2):
        spread_start(xs, g1, h, 0)
        own_piece(xs, g1, h)
    halo_begin(slab, tail, 0)
    halo_middle(slab, tail, 0)
    halo_wait(slab, tail, 0)
    apply_band(vf_ref, slab)
    mix(False)

    modes[WAVES:WAVES_PAD, :] = jnp.zeros((WAVES_PAD - WAVES, LANES), BF16)
    modes[WAVES_PAD + WAVES :, :] = jnp.zeros((WAVES_PAD - WAVES, LANES), BF16)
    STEP = 144
    for copy in table_copies:
        copy.wait()

    for h in range(2):
        lanes = slice(h * LANES, (h + 1) * LANES)
        spread_wait(g1, h, 0)
        to_spectrum(0, g1, h, spectrum.at[h])

        def gain(n, carry):
            low = pl.ds(pl.multiple_of(n * STEP, 16), STEP)
            high = pl.ds(pl.multiple_of(WAVES_PAD + n * STEP, 16), STEP)
            real_part, imag_part = spectrum[h, low, :], spectrum[h, high, :]
            real_gain, imag_gain = sf_ref[0, low, lanes], sf_ref[1, low, lanes]
            modes[low, :] = (real_gain * real_part - imag_gain * imag_part).astype(BF16)
            modes[high, :] = (real_gain * imag_part + imag_gain * real_part).astype(BF16)
            return carry

        lax.fori_loop(0, WAVES // STEP, gain, 0)
        to_field(1, ys, h)
        spread_start(ys, s1, h, 1)
        own_piece(ys, s1, h)

    for h in range(2):
        lanes = slice(h * LANES, (h + 1) * LANES)
        spread_wait(s1, h, 1)

        def activate(i, carry):
            preact = dense[i, :, lanes] + s1[h, i].astype(F32)
            logistic = 1.0 / (1.0 + jnp.exp(-preact))
            own = slab[i + 1, 0:PAD, lanes].astype(F32)
            out_ref[i, :, lanes] = (own + preact * logistic).astype(BF16)
            slope = logistic * (1.0 + preact * (1.0 - logistic))
            grad = (cts[i, :, lanes].astype(F32) * slope).astype(BF16)
            ps[h, i] = grad
            pslab[i + 1, 0:PAD, lanes] = grad
            return carry

        lax.fori_loop(0, ROWS, activate, 0)
        spread_start(ps, g2, h, 2)
        own_piece(ps, g2, h)

    halo_begin(pslab, ptail, 8)

    for k in range(3):
        total = jnp.zeros((CHANNELS, CHANNELS), F32)
        part = lax.dot_general(
            resp[k].reshape(ROWS * PAD, CHANNELS),
            pslab[1:17, 0:PAD, :].reshape(ROWS * PAD, CHANNELS),
            (((0,), (0,)), ((), ())),
            preferred_element_type=F32,
        )
        ws[16 * k : 16 * (k + 1)] = part.astype(BF16).reshape(16, 16, CHANNELS)

    def lat_spread(source, target, index):
        def body(step, carry):
            peer = lax.rem(lat + step, ROWS)
            pltpu.make_async_remote_copy(
                src_ref=source(peer),
                dst_ref=target,
                send_sem=ar_send.at[index],
                recv_sem=ar_recv.at[index],
                device_id={"lat": peer},
                device_id_type=MESH,
            ).start()
            return carry

        lax.fori_loop(1, ROWS, body, 0)

    lat_spread(lambda peer: ws.at[pl.ds(3 * peer, 3)], wr.at[lat], 0)
    wr[lat] = ws[pl.ds(3 * lat, 3)]
    halo_middle(pslab, ptail, 8)

    for h in range(2):
        lanes = slice(h * LANES, (h + 1) * LANES)
        spread_wait(g2, h, 2)
        cot_modes = cotspec
        to_spectrum(2, g2, h, cot_modes)
        fs[h, 45:48] = jnp.zeros((3, 16, LANES), BF16)
        fs[h, 93:96] = jnp.zeros((3, 16, LANES), BF16)

        def back(n, carry):
            low = pl.ds(pl.multiple_of(n * STEP, 16), STEP)
            high = pl.ds(pl.multiple_of(WAVES_PAD + n * STEP, 16), STEP)
            real_part, imag_part = spectrum[h, low, :], spectrum[h, high, :]
            real_cot, imag_cot = cot_modes[low, :], cot_modes[high, :]
            real_gain, imag_gain = sf_ref[0, low, lanes], sf_ref[1, low, lanes]
            modes[low, :] = (real_gain * real_cot + imag_gain * imag_cot).astype(BF16)
            modes[high, :] = (real_gain * imag_cot - imag_gain * real_cot).astype(BF16)
            first = real_cot * real_part + imag_cot * imag_part
            second = imag_cot * real_part - real_cot * imag_part
            fs[h, pl.ds(9 * n, 9)] = first.astype(BF16).reshape(9, 16, LANES)
            fs[h, pl.ds(48 + 9 * n, 9)] = second.astype(BF16).reshape(9, 16, LANES)
            return carry

        lax.fori_loop(0, WAVES // STEP, back, 0)
        to_field(3, zs, h)
        spread_start(zs, s2, h, 3)
        own_piece(zs, s2, h)
        lat_spread(lambda peer: fs.at[h, pl.ds(6 * peer, 6)], fr.at[h, lat], 1 + h)
        fr[h, lat] = fs[h, pl.ds(6 * lat, 6)]

    halo_wait(pslab, ptail, 8)
    apply_band(vb_ref, pslab)

    wait_bytes(wr.at[pl.ds(0, ROWS - 1)], ar_recv.at[0])
    w2s[...] = jnp.sum(wr[...].astype(F32), axis=0).astype(BF16)
    for h in range(2):
        wait_bytes(fr.at[h, pl.ds(0, ROWS - 1)], ar_recv.at[1 + h])
        f2s[6 * h : 6 * (h + 1)] = jnp.sum(fr[h].astype(F32), axis=0).astype(BF16)

    def to_owner(source, target, owner, index):
        @pl.when(me != owner)
        def _():
            pltpu.make_async_remote_copy(
                src_ref=source,
                dst_ref=target.at[me],
                send_sem=ar_send.at[index],
                recv_sem=ar_recv.at[index],
                device_id={"lon": owner},
                device_id_type=MESH,
            ).start()

    for o in range(12):
        to_owner(f2s.at[o], f2r, o, 3)
    for o in range(3):
        to_owner(w2s.at[o], w2r, 12 + o, 4)

    mix(True)

    def own_sum(source, work, target, slot, index, out_index):
        wait_bytes(work.at[pl.ds(0, ROWS - 1)], ar_recv.at[index])
        work[me] = source[slot]
        target[slot] = jnp.sum(work[...].astype(F32), axis=0).astype(BF16)

        def body(step, carry):
            peer = lax.rem(me + step, ROWS)
            pltpu.make_async_remote_copy(
                src_ref=target.at[slot],
                dst_ref=target.at[slot],
                send_sem=ar_send.at[out_index],
                recv_sem=ar_recv.at[out_index],
                device_id={"lon": peer},
                device_id_type=MESH,
            ).start()
            return carry

        lax.fori_loop(1, ROWS, body, 0)

    is_f = me < 12
    is_w = (me >= 12) & (me < 15)

    @pl.when(is_f)
    def _():
        own_sum(f2s, f2r, f3, me, 3, 5)

    @pl.when(is_w)
    def _():
        own_sum(w2s, w2r, w3, me - 12, 4, 6)

    def finish(h):
        lanes = slice(h * LANES, (h + 1) * LANES)
        spread_wait(s2, h, 3)

        def body(i, carry):
            value = dense[i, :, lanes] + s2[h, i].astype(F32)
            gin_ref[i, :, lanes] = (cts[i, :, lanes].astype(F32) + value).astype(BF16)
            return carry

        lax.fori_loop(0, ROWS, body, 0)

    finish(0)

    @pl.when(is_f)
    def _():
        wait_bytes(f3.at[pl.ds(0, 11)], ar_recv.at[5])

    @pl.when(jnp.logical_not(is_f))
    def _():
        wait_bytes(f3, ar_recv.at[5])

    @pl.when(is_w)
    def _():
        wait_bytes(w3.at[pl.ds(0, 2)], ar_recv.at[6])

    @pl.when(jnp.logical_not(is_w))
    def _():
        wait_bytes(w3, ar_recv.at[6])

    lat_spread(lambda peer: f3, ffin.at[lat], 7)
    lat_spread(lambda peer: w3, wfin.at[lat], 8)
    ffin[lat] = f3[...]
    wfin[lat] = w3[...]

    finish(1)

    wait_bytes(wfin.at[pl.ds(0, ROWS - 1)], ar_recv.at[8])
    gw_ref[...] = wfin[...].reshape(3 * CHANNELS, CHANNELS)
    wait_bytes(ffin.at[pl.ds(0, ROWS - 1)], ar_recv.at[7])

    def unpack(s, carry):
        rows = pl.ds(pl.multiple_of(s * PAD, PAD), PAD)
        for h in range(2):
            gf_ref[rows, h * LANES : (h + 1) * LANES] = ffin[s, 6 * h : 6 * (h + 1)].reshape(
                PAD, LANES
            )
        return carry

    lax.fori_loop(0, ROWS, unpack, 0)

    for phase, source in enumerate((xs, ys, ps, zs)):
        for h in range(2):
            wait_bytes(source.at[h, pl.ds(0, ROWS - 1)], a_send.at[phase, h])
    halo_end(slab, tail, 0)
    halo_end(pslab, ptail, 8)
    wait_bytes(wr.at[pl.ds(0, ROWS - 1)], ar_send.at[0])
    for h in range(2):
        wait_bytes(fr.at[h, pl.ds(0, ROWS - 1)], ar_send.at[1 + h])

    @pl.when(is_f)
    def _():
        wait_bytes(f2s.at[pl.ds(0, 11)], ar_send.at[3])
        wait_bytes(f2r.at[pl.ds(0, ROWS - 1)], ar_send.at[5])

    @pl.when(jnp.logical_not(is_f))
    def _():
        wait_bytes(f2s, ar_send.at[3])

    @pl.when(is_w)
    def _():
        wait_bytes(w2s.at[pl.ds(0, 2)], ar_send.at[4])
        wait_bytes(w2r.at[pl.ds(0, ROWS - 1)], ar_send.at[6])

    @pl.when(jnp.logical_not(is_w))
    def _():
        wait_bytes(w2s, ar_send.at[4])

    wait_bytes(ffin.at[pl.ds(0, ROWS - 1)], ar_send.at[7])
    wait_bytes(wfin.at[pl.ds(0, ROWS - 1)], ar_send.at[8])


def circular(vectors):
    ahead, behind = vectors[..., SPREAD:], vectors[..., :SPREAD]
    gap = jnp.zeros(vectors.shape[:-1] + (WIDE - 2 * SPREAD - 1,), vectors.dtype)
    return jnp.concatenate([ahead, gap, behind], axis=-1)


def on_device(features, cotangent, disco_basis, support_width, mix_weight, spectral_filter):
    effective = masked_basis(disco_basis, support_width).astype(F32)
    padded_basis = jnp.pad(effective, ((0, 0), (1, 1), (0, 0), (0, 0)))
    local = lax.dynamic_slice_in_dim(padded_basis, lax.axis_index("lat") * ROWS, ROWS + 2, 1)
    ahead = jnp.transpose(local[:, 1 : ROWS + 1], (1, 0, 2, 3))
    behind = jnp.stack([local[:, r : r + ROWS, 2 - r, ::-1] for r in range(3)], axis=2)
    behind = jnp.transpose(behind, (1, 0, 2, 3))
    ahead = circular(ahead).reshape(ROWS, 9, WIDE)
    behind = circular(behind).reshape(ROWS, 9, WIDE)
    tables = [jnp.asarray(t) for t in dft_tables()]

    vmem = pl.BlockSpec(memory_space=pltpu.VMEM)
    hbm = pl.BlockSpec(memory_space=pl.ANY)
    pieces = (2, ROWS, PAD, LANES)
    out, gin, gw, gf = pl.pallas_call(
        kernel,
        out_shape=[
            jax.ShapeDtypeStruct((ROWS, PAD, CHANNELS), BF16),
            jax.ShapeDtypeStruct((ROWS, PAD, CHANNELS), BF16),
            jax.ShapeDtypeStruct((3 * CHANNELS, CHANNELS), BF16),
            jax.ShapeDtypeStruct((2 * WAVES_PAD, CHANNELS), BF16),
        ],
        in_specs=[vmem] * 6 + [hbm] * 4,
        out_specs=[vmem] * 4,
        scratch_shapes=[
            pltpu.VMEM((4, ROWS * PAD, ROWS * PAD), BF16),
            pltpu.VMEM((ROWS, PAD, CHANNELS), BF16),
            pltpu.VMEM((ROWS + 2, WIDE, CHANNELS), BF16),
            pltpu.VMEM((ROWS + 2, WIDE, CHANNELS), BF16),
            pltpu.VMEM((ROWS + 2, SPREAD, CHANNELS), BF16),
            pltpu.VMEM((ROWS + 2, SPREAD, CHANNELS), BF16),
        ]
        + [pltpu.VMEM(pieces, BF16)] * 8
        + [
            pltpu.VMEM((3, ROWS, PAD, CHANNELS), BF16),
            pltpu.VMEM((ROWS, PAD, CHANNELS), F32),
            pltpu.VMEM((2, 2 * WAVES_PAD, LANES), F32),
            pltpu.VMEM((2 * WAVES_PAD, LANES), F32),
            pltpu.VMEM((2 * WAVES_PAD, LANES), BF16),
            pltpu.VMEM((3 * PAD, 3 * WIDE), BF16),
            pltpu.VMEM((48, 16, CHANNELS), BF16),
            pltpu.VMEM((ROWS, 3, 16, CHANNELS), BF16),
            pltpu.VMEM((3, 16, CHANNELS), BF16),
            pltpu.VMEM((ROWS, 16, CHANNELS), BF16),
            pltpu.VMEM((3, 16, CHANNELS), BF16),
            pltpu.VMEM((ROWS, 3, 16, CHANNELS), BF16),
            pltpu.VMEM((2, 96, 16, LANES), BF16),
            pltpu.VMEM((2, ROWS, 6, 16, LANES), BF16),
            pltpu.VMEM((12, 16, LANES), BF16),
            pltpu.VMEM((ROWS, 16, LANES), BF16),
            pltpu.VMEM((12, 16, LANES), BF16),
            pltpu.VMEM((ROWS, 12, 16, LANES), BF16),
            pltpu.SemaphoreType.DMA((4,)),
            pltpu.SemaphoreType.DMA((4, 2)),
            pltpu.SemaphoreType.DMA((4, 2)),
            pltpu.SemaphoreType.DMA((16,)),
            pltpu.SemaphoreType.DMA((16,)),
            pltpu.SemaphoreType.DMA((9,)),
            pltpu.SemaphoreType.DMA((9,)),
        ],
        compiler_params=pltpu.CompilerParams(
            collective_id=0, has_side_effects=True, vmem_limit_bytes=60 * 1024 * 1024
        ),
        cost_estimate=pl.CostEstimate(
            flops=8_000_000_000, bytes_accessed=30_000_000, transcendentals=400_000
        ),
    )(features, cotangent, ahead, behind, mix_weight, spectral_filter, *tables)
    return (
        out[:, :COLS],
        gin[:, :COLS],
        gw.astype(F32).reshape(3, CHANNELS, CHANNELS),
        gf.reshape(2, WAVES_PAD, CHANNELS)[:, :WAVES].astype(F32),
    )


def solution(mesh):
    return jax.shard_map(
        on_device,
        mesh=mesh,
        in_specs=(P("lat", "lon", None), P("lat", "lon", None), P(), P(), P(), P()),
        out_specs=(P("lat", "lon", None), P("lat", "lon", None), P(), P()),
        check_vma=False,
    )
```

```python
import math

import jax
import jax.numpy as jnp
import ml_dtypes
import numpy as np
from jax import lax
from jax.experimental import pallas as pl
from jax.experimental.pallas import tpu as pltpu
from jax.sharding import PartitionSpec as P

MESH = pl.DeviceIdType.MESH
F32 = jnp.float32
BF16 = jnp.bfloat16

ROWS = 16
COLS = 90
PAD = 96
WAVES = 720
WAVES_PAD = 768
SPREAD = 16
LANES = 128
CHANNELS = 256
WIDE = 128
TILE = 384


def dft_tables():
    longitudes = ROWS * COLS
    cell_index = np.arange(longitudes, dtype=np.int64)
    wave_index = np.arange(WAVES, dtype=np.int64)
    phase_index = wave_index[:, None] * cell_index[None, :] % longitudes
    angles = phase_index.astype(np.float32) * np.float32(2.0 * math.pi / longitudes)
    cosine_wave = np.cos(angles)
    sine_wave = np.sin(angles)
    factor = np.where(wave_index == 0, 1.0, 2.0).astype(np.float32) / np.float32(longitudes)

    def padded(real, imag):
        table = np.zeros((2, WAVES_PAD, ROWS, PAD), np.float32)
        table[0, :WAVES, :, :COLS] = real.reshape(WAVES, ROWS, COLS)
        table[1, :WAVES, :, :COLS] = imag.reshape(WAVES, ROWS, COLS)
        return table.reshape(2 * WAVES_PAD, ROWS * PAD).astype(ml_dtypes.bfloat16)

    forward = padded(cosine_wave, -sine_wave)
    inverse_t = padded(cosine_wave * factor[:, None], -sine_wave * factor[:, None])
    return (
        forward,
        np.ascontiguousarray(inverse_t.T),
        inverse_t,
        np.ascontiguousarray(forward.T),
    )


def kernel(
    x_ref, ct_ref, basis_ref, width_ref, mix_ref, sf_ref, t0_ref, t1_ref, t2_ref, t3_ref,
    out_ref, gin_ref, gw_ref, gf_ref,
    tables, ctv, mixv, sfv, perm, vf, vb, cts, slab, pslab, tail, ptail,
    xs, g1, ys, s1, ps, g2, zs, s2,
    resp, dense, spectrum, cotspec, modes, band, outs, folded, gfold,
    parts, pair_in, pair_sum, lat_in, lat_sum, z_in, total,
    load_sem, store_sem, a_send, a_recv, halo_send, halo_recv, ar_send, ar_recv,
):
    me = lax.axis_index("lon")
    lat = lax.axis_index("lat")
    right = lax.rem(me + 1, ROWS)
    left = lax.rem(me + ROWS - 1, ROWS)
    core = lax.rem(me, 2)
    chip = lax.div(me, 2)
    twin = me + 1 - 2 * core

    loads = [
        pltpu.make_async_copy(ref, target, load_sem.at[i])
        for i, (ref, target) in enumerate(
            (
                (ct_ref, ctv),
                (t0_ref, tables.at[0]),
                (sf_ref, sfv),
                (t1_ref, tables.at[1]),
                (mix_ref, mixv),
                (t2_ref, tables.at[2]),
                (t3_ref, tables.at[3]),
            )
        )
    ]
    for copy in loads:
        copy.start()

    barrier = pltpu.get_barrier_semaphore()

    def greet(step, carry):
        pl.semaphore_signal(
            barrier, inc=1, device_id={"lon": lax.rem(me + step, ROWS)}, device_id_type=MESH
        )
        pl.semaphore_signal(
            barrier, inc=1, device_id={"lat": lax.rem(lat + step, ROWS)}, device_id_type=MESH
        )
        return carry

    lax.fori_loop(1, ROWS, greet, 0)

    a = lax.broadcasted_iota(jnp.int32, (256, 256), 0)
    b = lax.broadcasted_iota(jnp.int32, (256, 256), 1)
    perm[...] = jnp.where(b == (a & 15) * 16 + (a >> 4), 1.0, 0.0).astype(BF16)

    def unfold(source, store):
        for g in range(6):
            count = min(16, COLS - 16 * g)
            data = source[16 * g : 16 * g + count].reshape(count * ROWS, CHANNELS)
            value = jnp.dot(perm[:, 0 : count * ROWS], data, preferred_element_type=F32)
            store(slice(16 * g, 16 * g + 16), value.astype(BF16).reshape(ROWS, 16, CHANNELS))

    def fold(source, target, lanes):
        for g in range(6):
            count = min(16, COLS - 16 * g)
            data = source[:, 16 * g : 16 * g + 16, lanes]
            width = data.shape[2]
            value = jnp.dot(perm[...], data.reshape(256, width), preferred_element_type=F32)
            value = value.astype(BF16).reshape(16, ROWS, width)
            target[16 * g : 16 * g + count, :, lanes] = value[0:count]

    def store_x(columns, value):
        slab[1:17, columns, :] = value
        for h in range(2):
            xs[h, :, columns, :] = value[:, :, h * LANES : (h + 1) * LANES]

    def store_ct(columns, value):
        cts[:, columns, :] = value

    unfold(x_ref, store_x)
    pl.semaphore_wait(barrier, 2 * (ROWS - 1))

    def offset(step):
        return 8 + (1 - 2 * lax.rem(step, 2)) * lax.div(step + 1, 2)

    def spread_start(source, target, h, phase, first=0, end=ROWS - 1):
        def body(step, carry):
            peer = lax.rem(me + offset(step), ROWS)
            pltpu.make_async_remote_copy(
                src_ref=source.at[h, peer],
                dst_ref=target.at[h, me],
                send_sem=a_send.at[phase, h],
                recv_sem=a_recv.at[phase, h],
                device_id={"lon": peer},
                device_id_type=MESH,
            ).start()
            return carry

        lax.fori_loop(first, end, body, 0)

    def own_piece(source, target, h):
        target[h, me] = source[h, me]

    def wait_bytes(ref, sem):
        pltpu.make_async_copy(ref, ref, sem).wait()

    def spread_wait(target, h, phase):
        wait_bytes(target.at[h, pl.ds(0, ROWS - 1)], a_recv.at[phase, h])

    def halo_copy(src, dst, index, device):
        return pltpu.make_async_remote_copy(
            src_ref=src,
            dst_ref=dst,
            send_sem=halo_send.at[index],
            recv_sem=halo_recv.at[index],
            device_id=device,
            device_id_type=MESH,
        )

    def lat_halo(buf, base):
        up = halo_copy(
            buf.at[1, pl.ds(0, PAD)], buf.at[17, pl.ds(0, PAD)], base, {"lat": lax.max(lat - 1, 0)}
        )
        down = halo_copy(
            buf.at[16, pl.ds(0, PAD)],
            buf.at[0, pl.ds(0, PAD)],
            base + 1,
            {"lat": lax.min(lat + 1, ROWS - 1)},
        )
        return up, down

    def lon_halo(buf, end, base):
        pairs = []
        for n, rows in enumerate((pl.ds(1, ROWS), pl.ds(0, 1), pl.ds(17, 1))):
            pairs.append(
                (
                    halo_copy(
                        buf.at[rows, pl.ds(0, SPREAD)],
                        buf.at[rows, pl.ds(PAD, SPREAD)],
                        base + 2 + 2 * n,
                        {"lon": left},
                    ),
                    halo_copy(
                        end.at[rows],
                        buf.at[rows, pl.ds(PAD + SPREAD, SPREAD)],
                        base + 3 + 2 * n,
                        {"lon": right},
                    ),
                )
            )
        return pairs

    def tail_row(buf, end, i):
        moved = pltpu.roll(buf[i, 0:PAD, :].astype(F32), PAD - COLS, 0)
        end[i] = moved[PAD - SPREAD : PAD].astype(BF16)

    def halo_begin(buf, end, base):
        up, down = lat_halo(buf, base)

        @pl.when(lat > 0)
        def _():
            up.start()

        @pl.when(lat < ROWS - 1)
        def _():
            down.start()

        def body(i, carry):
            tail_row(buf, end, i + 1)
            return carry

        lax.fori_loop(0, ROWS, body, 0)
        for copy in lon_halo(buf, end, base)[0]:
            copy.start()

    def halo_middle(buf, end, base):
        up, down = lat_halo(buf, base)

        @pl.when(lat > 0)
        def _():
            down.wait_recv()

        @pl.when(lat == 0)
        def _():
            buf[0, 0:PAD, :] = jnp.zeros((PAD, CHANNELS), BF16)

        @pl.when(lat < ROWS - 1)
        def _():
            up.wait_recv()

        @pl.when(lat == ROWS - 1)
        def _():
            buf[17, 0:PAD, :] = jnp.zeros((PAD, CHANNELS), BF16)

        tail_row(buf, end, 0)
        tail_row(buf, end, 17)
        for pair in lon_halo(buf, end, base)[1:]:
            for copy in pair:
                copy.start()

    def halo_wait_main(buf, end, base):
        for copy in lon_halo(buf, end, base)[0]:
            copy.wait_recv()

    def halo_wait_edge(buf, end, base):
        for pair in lon_halo(buf, end, base)[1:]:
            for copy in pair:
                copy.wait_recv()

    def halo_end(buf, end, base):
        up, down = lat_halo(buf, base)

        @pl.when(lat > 0)
        def _():
            up.wait_send()

        @pl.when(lat < ROWS - 1)
        def _():
            down.wait_send()

        for pair in lon_halo(buf, end, base):
            for copy in pair:
                copy.wait_send()

    lane = lax.broadcasted_iota(jnp.int32, (PAD, WIDE), 1)
    row = lax.broadcasted_iota(jnp.int32, (PAD, WIDE), 0)
    direct = (row < COLS) & ((lane < COLS) | (lane >= PAD + SPREAD))
    shifted = (row < COLS) & (lane >= PAD) & (lane < PAD + SPREAD)

    def band_row(vecs, buf, i, backward):
        for k in range(3):
            for r in range(3):
                if backward:
                    vec = vecs[3 * k + 2 - r, pl.ds(i + r, 1), :]
                else:
                    vec = vecs[3 * k + r, pl.ds(i + 1, 1), :]
                near = pltpu.roll(jnp.broadcast_to(vec, (PAD, WIDE)), 0, 1, stride=1, stride_axis=0)
                far = pltpu.roll(
                    jnp.broadcast_to(vec, (32, WIDE)), 64 + PAD - COLS, 1, stride=1, stride_axis=0
                )
                high = jnp.where(direct[64:], near[64:], jnp.where(shifted[64:], far, 0.0))
                lanes = slice(r * WIDE, (r + 1) * WIDE)
                band[k * PAD : k * PAD + 64, lanes] = jnp.where(direct[:64], near[:64], 0.0).astype(
                    BF16
                )
                band[k * PAD + 64 : (k + 1) * PAD, lanes] = high.astype(BF16)
        around = buf[pl.ds(i, 3)].reshape(3 * WIDE, CHANNELS)
        value = jnp.dot(band[...], around, preferred_element_type=F32).astype(BF16)
        for k in range(3):
            resp[k, i] = value[k * PAD : (k + 1) * PAD]

    def inner_rows(vecs, buf, backward):
        def body(i, carry):
            band_row(vecs, buf, i, backward)
            return carry

        lax.fori_loop(1, ROWS - 1, body, 0)

    def edge_rows(vecs, buf, backward):
        def body(n, carry):
            band_row(vecs, buf, n * (ROWS - 1), backward)
            return carry

        lax.fori_loop(0, 2, body, 0)

    def tap_vectors():
        offsets = jnp.abs(lax.broadcasted_iota(jnp.int32, (33, 256), 0) - SPREAD)
        retained = offsets <= width_ref[...]
        first = lax.broadcasted_iota(jnp.int32, (32, 256), 0) + lat * ROWS - 1
        chosen = jnp.where(lax.broadcasted_iota(jnp.int32, (32, 256), 1) == first, 1.0, 0.0)
        tap = lax.broadcasted_iota(jnp.int32, (33, WIDE), 0)
        spot = lax.broadcasted_iota(jnp.int32, (33, WIDE), 1)
        ahead = jnp.where(((tap + WIDE - SPREAD) & (WIDE - 1)) == spot, 1.0, 0.0).astype(BF16)
        behind = jnp.where(((WIDE + SPREAD - tap) & (WIDE - 1)) == spot, 1.0, 0.0).astype(BF16)
        for k in range(3):
            for r in range(3):
                kept = jnp.where(retained, basis_ref[k, r].astype(F32), 0.0).astype(BF16)
                local = lax.dot_general(
                    chosen.astype(BF16), kept, (((1,), (1,)), ((), ())), preferred_element_type=F32
                ).astype(BF16)
                vf[3 * k + r] = jnp.dot(local, ahead, preferred_element_type=F32)
                vb[3 * k + r] = jnp.dot(local, behind, preferred_element_type=F32)

    def mix(transposed):
        def body(n, carry):
            total = jnp.zeros((TILE, CHANNELS), F32)
            for k in range(3):
                part = resp[k, pl.ds(4 * n, 4)].reshape(TILE, CHANNELS)
                total = total + lax.dot_general(
                    part,
                    mixv[k],
                    (((1,), (1 if transposed else 0,)), ((), ())),
                    preferred_element_type=F32,
                )
            dense[pl.ds(4 * n, 4)] = total.reshape(4, PAD, CHANNELS)
            return carry

        lax.fori_loop(0, 4, body, 0)

    def to_spectrum(table, field, h, target):
        def body(n, carry):
            rows = pl.ds(pl.multiple_of(n * TILE, TILE), TILE)
            target[rows, :] = jnp.dot(
                tables[table, rows, :],
                field[h].reshape(ROWS * PAD, LANES),
                preferred_element_type=F32,
            )
            return carry

        lax.fori_loop(0, 4, body, 0)

    def to_field(table, field, h):
        def body(n, carry):
            rows = pl.ds(pl.multiple_of(n * TILE, TILE), TILE)
            value = jnp.dot(tables[table, rows, :], modes[...], preferred_element_type=F32)
            field[h, pl.ds(4 * n, 4)] = value.astype(BF16).reshape(4, PAD, LANES)
            return carry

        lax.fori_loop(0, 4, body, 0)

    def chunk_start(source, target, stage, q, device):
        pltpu.make_async_remote_copy(
            src_ref=source,
            dst_ref=target,
            send_sem=ar_send.at[stage, q],
            recv_sem=ar_recv.at[stage, q],
            device_id=device,
            device_id_type=MESH,
        ).start()

    def pair_start(q):
        chunk_start(parts.at[q, 1 - core], pair_in.at[q], 0, q, {"lon": twin})

    def to_lat(source, target, stage, q):
        def body(step, carry):
            peer = lax.rem(lat + step, ROWS)
            chunk_start(source(peer), target, stage, q, {"lat": peer})
            return carry

        lax.fori_loop(1, ROWS, body, 0)

    def pair_finish(q):
        wait_bytes(pair_in.at[q], ar_recv.at[0, q])

        def body(n, carry):
            rows = pl.ds(6 * n, 6)
            both = parts[q, core, rows].astype(F32) + pair_in[q, rows].astype(F32)
            pair_sum[q, rows] = both.astype(BF16)
            return carry

        lax.fori_loop(0, 8, body, 0)
        to_lat(lambda peer: pair_sum.at[q, pl.ds(3 * peer, 3)], lat_in.at[q, lat], 1, q)
        lat_in[q, lat] = pair_sum[q, pl.ds(3 * lat, 3)]

    def lat_finish(q):
        wait_bytes(lat_in.at[q, pl.ds(0, ROWS - 1)], ar_recv.at[1, q])
        value = jnp.sum(lat_in[q].astype(F32), axis=0).astype(BF16)
        lat_sum[q] = value
        z_in[q, chip] = value

        def body(step, carry):
            peer = lax.rem(me + 2 * step, ROWS)
            chunk_start(lat_sum.at[q], z_in.at[q, chip], 2, q, {"lon": peer})
            return carry

        lax.fori_loop(1, ROWS // 2, body, 0)

    def z_finish(q):
        wait_bytes(z_in.at[q, pl.ds(0, ROWS // 2 - 1)], ar_recv.at[2, q])
        mine = pl.ds(3 * lat, 3)
        total[q, core, mine] = jnp.sum(z_in[q].astype(F32), axis=0).astype(BF16)
        to_lat(lambda peer: total.at[q, core, mine], total.at[q, core, mine], 3, q)

    def gather_finish(q):
        wait_bytes(total.at[q, 0, pl.ds(0, 45)], ar_recv.at[3, q])
        chunk_start(total.at[q, core], total.at[q, core], 4, q, {"lon": twin})

    def chunk_wait(q):
        wait_bytes(total.at[q, 0], ar_recv.at[4, q])

    def chunk_end(q):
        wait_bytes(total.at[q, 0], ar_send.at[0, q])
        wait_bytes(total.at[q, 0, pl.ds(0, 45)], ar_send.at[1, q])
        wait_bytes(total.at[q, 0, pl.ds(0, 21)], ar_send.at[2, q])
        wait_bytes(total.at[q, 0, pl.ds(0, 45)], ar_send.at[3, q])
        wait_bytes(total.at[q, 0], ar_send.at[4, q])

    spread_start(xs, g1, 0, 0)
    halo_begin(slab, tail, 0)
    spread_start(xs, g1, 1, 0)
    for h in range(2):
        own_piece(xs, g1, h)
    tap_vectors()
    loads[0].wait()
    unfold(ctv, store_ct)
    modes[WAVES:WAVES_PAD, :] = jnp.zeros((WAVES_PAD - WAVES, LANES), BF16)
    modes[WAVES_PAD + WAVES :, :] = jnp.zeros((WAVES_PAD - WAVES, LANES), BF16)
    for h in range(2):
        for c in range(2):
            parts[1 + h, c, 45:48] = jnp.zeros((3, 16, LANES), BF16)
    halo_middle(slab, tail, 0)
    STEP = 144
    for copy in loads[1:]:
        copy.wait()

    for h in range(2):
        lanes = slice(h * LANES, (h + 1) * LANES)
        spread_wait(g1, h, 0)
        to_spectrum(0, g1, h, spectrum.at[h])

        def gain(n, carry):
            low = pl.ds(pl.multiple_of(n * STEP, 16), STEP)
            high = pl.ds(pl.multiple_of(WAVES_PAD + n * STEP, 16), STEP)
            real_part, imag_part = spectrum[h, low, :], spectrum[h, high, :]
            real_gain, imag_gain = sfv[0, low, lanes], sfv[1, low, lanes]
            modes[low, :] = (real_gain * real_part - imag_gain * imag_part).astype(BF16)
            modes[high, :] = (real_gain * imag_part + imag_gain * real_part).astype(BF16)
            return carry

        lax.fori_loop(0, WAVES // STEP, gain, 0)
        to_field(1, ys, h)
        spread_start(ys, s1, h, 1)
        own_piece(ys, s1, h)
        if h == 0:
            halo_wait_main(slab, tail, 0)
            inner_rows(vf, slab, False)

    halo_wait_edge(slab, tail, 0)
    edge_rows(vf, slab, False)
    mix(False)

    for h in range(2):
        lanes = slice(h * LANES, (h + 1) * LANES)
        spread_wait(s1, h, 1)

        def activate(i, carry):
            preact = dense[i, :, lanes] + s1[h, i].astype(F32)
            logistic = 1.0 / (1.0 + jnp.exp(-preact))
            own = slab[i + 1, 0:PAD, lanes].astype(F32)
            outs[i, :, lanes] = (own + preact * logistic).astype(BF16)
            slope = logistic * (1.0 + preact * (1.0 - logistic))
            grad = (cts[i, :, lanes].astype(F32) * slope).astype(BF16)
            ps[h, i] = grad
            pslab[i + 1, 0:PAD, lanes] = grad
            return carry

        lax.fori_loop(0, ROWS, activate, 0)
        if h == 1:
            halo_begin(pslab, ptail, 8)
        spread_start(ps, g2, h, 2)
        own_piece(ps, g2, h)

    for k in range(3):
        part = lax.dot_general(
            resp[k].reshape(ROWS * PAD, CHANNELS),
            pslab[1:17, 0:PAD, :].reshape(ROWS * PAD, CHANNELS),
            (((0,), (0,)), ((), ())),
            preferred_element_type=F32,
        ).astype(BF16)
        for c in range(2):
            parts[0, c, 16 * k : 16 * (k + 1)] = part[:, c * LANES : (c + 1) * LANES].reshape(
                16, 16, LANES
            )
    pair_start(0)
    halo_middle(pslab, ptail, 8)
    fold(outs, folded, slice(0, CHANNELS))
    out_store = pltpu.make_async_copy(folded, out_ref, store_sem.at[0])
    out_store.start()

    for h in range(2):
        lanes = slice(h * LANES, (h + 1) * LANES)
        spread_wait(g2, h, 2)
        to_spectrum(2, g2, h, cotspec)

        def back(n, carry):
            low = pl.ds(pl.multiple_of(n * STEP, 16), STEP)
            high = pl.ds(pl.multiple_of(WAVES_PAD + n * STEP, 16), STEP)
            real_part, imag_part = spectrum[h, low, :], spectrum[h, high, :]
            real_cot, imag_cot = cotspec[low, :], cotspec[high, :]
            real_gain, imag_gain = sfv[0, low, lanes], sfv[1, low, lanes]
            modes[low, :] = (real_gain * real_cot + imag_gain * imag_cot).astype(BF16)
            modes[high, :] = (real_gain * imag_cot - imag_gain * real_cot).astype(BF16)
            first = real_cot * real_part + imag_cot * imag_part
            second = imag_cot * real_part - real_cot * imag_part
            parts[1 + h, 0, pl.ds(9 * n, 9)] = first.astype(BF16).reshape(9, 16, LANES)
            parts[1 + h, 1, pl.ds(9 * n, 9)] = second.astype(BF16).reshape(9, 16, LANES)
            return carry

        lax.fori_loop(0, WAVES // STEP, back, 0)
        pair_start(1 + h)
        if h == 0:
            pair_finish(0)
        to_field(3, zs, h)
        if h == 0:
            spread_start(zs, s2, h, 3)
            own_piece(zs, s2, h)
            pair_finish(1)
            halo_wait_main(pslab, ptail, 8)
            inner_rows(vb, pslab, True)
            lat_finish(0)
        else:
            pair_finish(2)
            spread_start(zs, s2, h, 3, 0, 8)
            own_piece(zs, s2, h)

    lat_finish(1)
    halo_wait_edge(pslab, ptail, 8)
    edge_rows(vb, pslab, True)
    lat_finish(2)
    spread_start(zs, s2, 1, 3, 8, ROWS - 1)
    mix(True)
    z_finish(0)

    def finish(h):
        lanes = slice(h * LANES, (h + 1) * LANES)
        spread_wait(s2, h, 3)

        def body(i, carry):
            value = dense[i, :, lanes] + s2[h, i].astype(F32)
            outs[i, :, lanes] = (cts[i, :, lanes].astype(F32) + value).astype(BF16)
            return carry

        lax.fori_loop(0, ROWS, body, 0)
        fold(outs, gfold, lanes)
        store = pltpu.make_async_copy(
            gfold.at[:, :, lanes], gin_ref.at[:, :, lanes], store_sem.at[1 + h]
        )
        store.start()
        return store

    z_finish(1)
    finals = [finish(0)]
    z_finish(2)
    gather_finish(0)
    gather_finish(1)
    chunk_wait(0)
    for k in range(3):
        for c in range(2):
            gw_ref[k, :, c * LANES : (c + 1) * LANES] = (
                total[0, c, 16 * k : 16 * (k + 1)].reshape(CHANNELS, LANES).astype(F32)
            )
    def filter_out(h):
        chunk_wait(1 + h)
        for c in range(2):
            gf_ref[c, :, h * LANES : (h + 1) * LANES] = (
                total[1 + h, c, 0:45].reshape(WAVES, LANES).astype(F32)
            )

    filter_out(0)
    gather_finish(2)
    finals.append(finish(1))
    filter_out(1)

    for phase, source in enumerate((xs, ys, ps, zs)):
        for h in range(2):
            wait_bytes(source.at[h, pl.ds(0, ROWS - 1)], a_send.at[phase, h])
    halo_end(slab, tail, 0)
    halo_end(pslab, ptail, 8)
    for q in range(3):
        chunk_end(q)
    out_store.wait()
    for store in finals:
        store.wait()


def deliver(*refs):
    sources, targets, held, arrived, left = refs[0:4], refs[4:8], refs[8:12], refs[12], refs[13]
    loads = [pltpu.make_async_copy(sources[i], held[i], arrived.at[i]) for i in range(4)]
    stores = [pltpu.make_async_copy(held[i], targets[i], left.at[i]) for i in range(4)]
    for copy in loads:
        copy.start()
    for i in range(4):
        loads[i].wait()
        stores[i].start()
    for copy in stores:
        copy.wait()


def on_device(features, cotangent, disco_basis, support_width, mix_weight, spectral_filter):
    tables = [jnp.asarray(t) for t in dft_tables()]
    vmem = pl.BlockSpec(memory_space=pltpu.VMEM)
    hbm = pl.BlockSpec(memory_space=pl.ANY)
    pieces = (2, ROWS, PAD, LANES)
    out, gin, gw, gf = pl.pallas_call(
        kernel,
        out_shape=[
            jax.ShapeDtypeStruct((COLS, ROWS, CHANNELS), BF16),
            jax.ShapeDtypeStruct((COLS, ROWS, CHANNELS), BF16),
            jax.ShapeDtypeStruct((3, CHANNELS, CHANNELS), F32),
            jax.ShapeDtypeStruct((2, WAVES, CHANNELS), F32),
        ],
        in_specs=[vmem, hbm, vmem, vmem] + [hbm] * 6,
        out_specs=[hbm, hbm, vmem, vmem],
        scratch_shapes=[
            pltpu.VMEM((4, ROWS * PAD, ROWS * PAD), BF16),
            pltpu.VMEM((COLS, ROWS, CHANNELS), BF16),
            pltpu.VMEM((3, CHANNELS, CHANNELS), BF16),
            pltpu.VMEM((2, WAVES, CHANNELS), F32),
            pltpu.VMEM((256, 256), BF16),
            pltpu.VMEM((9, 32, WIDE), F32),
            pltpu.VMEM((9, 32, WIDE), F32),
            pltpu.VMEM((ROWS, PAD, CHANNELS), BF16),
            pltpu.VMEM((ROWS + 2, WIDE, CHANNELS), BF16),
            pltpu.VMEM((ROWS + 2, WIDE, CHANNELS), BF16),
            pltpu.VMEM((ROWS + 2, SPREAD, CHANNELS), BF16),
            pltpu.VMEM((ROWS + 2, SPREAD, CHANNELS), BF16),
        ]
        + [pltpu.VMEM(pieces, BF16)] * 8
        + [
            pltpu.VMEM((3, ROWS, PAD, CHANNELS), BF16),
            pltpu.VMEM((ROWS, PAD, CHANNELS), F32),
            pltpu.VMEM((2, 2 * WAVES_PAD, LANES), F32),
            pltpu.VMEM((2 * WAVES_PAD, LANES), F32),
            pltpu.VMEM((2 * WAVES_PAD, LANES), BF16),
            pltpu.VMEM((3 * PAD, 3 * WIDE), BF16),
            pltpu.VMEM((ROWS, PAD, CHANNELS), BF16),
            pltpu.VMEM((COLS, ROWS, CHANNELS), BF16),
            pltpu.VMEM((COLS, ROWS, CHANNELS), BF16),
            pltpu.VMEM((3, 2, 48, 16, LANES), BF16),
            pltpu.VMEM((3, 48, 16, LANES), BF16),
            pltpu.VMEM((3, 48, 16, LANES), BF16),
            pltpu.VMEM((3, ROWS, 3, 16, LANES), BF16),
            pltpu.VMEM((3, 3, 16, LANES), BF16),
            pltpu.VMEM((3, ROWS // 2, 3, 16, LANES), BF16),
            pltpu.VMEM((3, 2, 48, 16, LANES), BF16),
            pltpu.SemaphoreType.DMA((7,)),
            pltpu.SemaphoreType.DMA((3,)),
            pltpu.SemaphoreType.DMA((4, 2)),
            pltpu.SemaphoreType.DMA((4, 2)),
            pltpu.SemaphoreType.DMA((16,)),
            pltpu.SemaphoreType.DMA((16,)),
            pltpu.SemaphoreType.DMA((5, 3)),
            pltpu.SemaphoreType.DMA((5, 3)),
        ],
        compiler_params=pltpu.CompilerParams(
            collective_id=0, has_side_effects=True, vmem_limit_bytes=60 * 1024 * 1024
        ),
        cost_estimate=pl.CostEstimate(
            flops=8_000_000_000, bytes_accessed=30_000_000, transcendentals=400_000
        ),
    )(
        jnp.transpose(features, (1, 0, 2)),
        jnp.transpose(cotangent, (1, 0, 2)),
        jnp.transpose(disco_basis, (0, 2, 3, 1)),
        support_width.reshape(1, -1),
        mix_weight,
        spectral_filter,
        *tables,
    )
    results = (out, gin, gw, gf)
    out, gin, gw, gf = pl.pallas_call(
        deliver,
        out_shape=[jax.ShapeDtypeStruct(r.shape, r.dtype) for r in results],
        in_specs=[hbm] * 4,
        out_specs=[hbm] * 4,
        scratch_shapes=[pltpu.VMEM(r.shape, r.dtype) for r in results]
        + [pltpu.SemaphoreType.DMA((4,)), pltpu.SemaphoreType.DMA((4,))],
    )(*results)
    return (jnp.transpose(out, (1, 0, 2)), jnp.transpose(gin, (1, 0, 2)), gw, gf)


def solution(mesh):
    return jax.shard_map(
        on_device,
        mesh=mesh,
        in_specs=(P("lat", "lon", None), P("lat", "lon", None), P(), P(), P(), P()),
        out_specs=(P("lat", "lon", None), P("lat", "lon", None), P(), P()),
        check_vma=False,
    )
```

```python
import math

import jax
import jax.numpy as jnp
import ml_dtypes
import numpy as np
from jax import lax
from jax.experimental import pallas as pl
from jax.experimental.pallas import tpu as pltpu
from jax.sharding import PartitionSpec as P

MESH = pl.DeviceIdType.MESH
F32 = jnp.float32
BF16 = jnp.bfloat16

ROWS = 16
COLS = 90
PAD = 96
WAVES = 720
WAVES_PAD = 768
SPREAD = 16
LANES = 128
CHANNELS = 256
WIDE = 128
TILE = 384
SCATTERED = (0,)


def dft_tables():
    longitudes = ROWS * COLS
    cell_index = np.arange(longitudes, dtype=np.int64)
    wave_index = np.arange(WAVES, dtype=np.int64)
    phase_index = wave_index[:, None] * cell_index[None, :] % longitudes
    angles = phase_index.astype(np.float32) * np.float32(2.0 * math.pi / longitudes)
    cosine_wave = np.cos(angles)
    sine_wave = np.sin(angles)
    factor = np.where(wave_index == 0, 1.0, 2.0).astype(np.float32) / np.float32(longitudes)

    def padded(real, imag):
        table = np.zeros((2, WAVES_PAD, ROWS, PAD), np.float32)
        table[0, :WAVES, :, :COLS] = real.reshape(WAVES, ROWS, COLS)
        table[1, :WAVES, :, :COLS] = imag.reshape(WAVES, ROWS, COLS)
        return table.reshape(2 * WAVES_PAD, ROWS * PAD).astype(ml_dtypes.bfloat16)

    forward = padded(cosine_wave, -sine_wave)
    inverse_t = padded(cosine_wave * factor[:, None], -sine_wave * factor[:, None])
    return (
        forward,
        np.ascontiguousarray(inverse_t.T),
        inverse_t,
        np.ascontiguousarray(forward.T),
    )


def kernel(
    x_ref, ct_ref, basis_ref, width_ref, mix_ref, sf_ref, t0_ref, t1_ref, t2_ref, t3_ref,
    out_ref, gin_ref, sum_ref,
    tables, ctv, mixv, sfv, perm, vf, vb, cts, slab, pslab, tail, ptail,
    xs, g1, ys, s1, ps, g2, zs, s2,
    resp, dense, spectrum, cotspec, modes, band, outs, folded, gfold,
    parts, pair_in, pair_sum, lat_in, lat_sum, z_in, z_tile, total,
    load_sem, store_sem, a_send, a_recv, halo_send, halo_recv, ar_send, ar_recv,
):
    me = lax.axis_index("lon")
    lat = lax.axis_index("lat")
    right = lax.rem(me + 1, ROWS)
    left = lax.rem(me + ROWS - 1, ROWS)
    core = lax.rem(me, 2)
    chip = lax.div(me, 2)
    twin = me + 1 - 2 * core

    loads = [
        pltpu.make_async_copy(ref, target, load_sem.at[i])
        for i, (ref, target) in enumerate(
            (
                (ct_ref, ctv),
                (t0_ref, tables.at[0]),
                (sf_ref, sfv),
                (t1_ref, tables.at[1]),
                (mix_ref, mixv),
                (t2_ref, tables.at[2]),
                (t3_ref, tables.at[3]),
            )
        )
    ]
    for copy in loads:
        copy.start()

    barrier = pltpu.get_barrier_semaphore()

    def greet(step, carry):
        pl.semaphore_signal(
            barrier, inc=1, device_id={"lon": lax.rem(me + step, ROWS)}, device_id_type=MESH
        )
        pl.semaphore_signal(
            barrier, inc=1, device_id={"lat": lax.rem(lat + step, ROWS)}, device_id_type=MESH
        )
        return carry

    lax.fori_loop(1, ROWS, greet, 0)

    a = lax.broadcasted_iota(jnp.int32, (256, 256), 0)
    b = lax.broadcasted_iota(jnp.int32, (256, 256), 1)
    perm[...] = jnp.where(b == (a & 15) * 16 + (a >> 4), 1.0, 0.0).astype(BF16)

    def unfold(source, store):
        for g in range(6):
            count = min(16, COLS - 16 * g)
            data = source[16 * g : 16 * g + count].reshape(count * ROWS, CHANNELS)
            value = jnp.dot(perm[:, 0 : count * ROWS], data, preferred_element_type=F32)
            store(slice(16 * g, 16 * g + 16), value.astype(BF16).reshape(ROWS, 16, CHANNELS))

    def fold(source, target, lanes):
        for g in range(6):
            count = min(16, COLS - 16 * g)
            data = source[:, 16 * g : 16 * g + 16, lanes]
            width = data.shape[2]
            value = jnp.dot(perm[...], data.reshape(256, width), preferred_element_type=F32)
            value = value.astype(BF16).reshape(16, ROWS, width)
            target[16 * g : 16 * g + count, :, lanes] = value[0:count]

    def store_x(columns, value):
        slab[1:17, columns, :] = value
        for h in range(2):
            xs[h, :, columns, :] = value[:, :, h * LANES : (h + 1) * LANES]

    def store_ct(columns, value):
        cts[:, columns, :] = value

    unfold(x_ref, store_x)
    pl.semaphore_wait(barrier, 2 * (ROWS - 1))

    def offset(step):
        return 8 + (1 - 2 * lax.rem(step, 2)) * lax.div(step + 1, 2)

    def spread_start(source, target, h, phase, first=0, end=ROWS - 1):
        def body(step, carry):
            peer = lax.rem(me + offset(step), ROWS)
            pltpu.make_async_remote_copy(
                src_ref=source.at[h, peer],
                dst_ref=target.at[h, me],
                send_sem=a_send.at[phase, h],
                recv_sem=a_recv.at[phase, h],
                device_id={"lon": peer},
                device_id_type=MESH,
            ).start()
            return carry

        lax.fori_loop(first, end, body, 0)

    def own_piece(source, target, h):
        target[h, me] = source[h, me]

    def wait_bytes(ref, sem):
        pltpu.make_async_copy(ref, ref, sem).wait()

    def spread_wait(target, h, phase):
        wait_bytes(target.at[h, pl.ds(0, ROWS - 1)], a_recv.at[phase, h])

    def halo_copy(src, dst, index, device):
        return pltpu.make_async_remote_copy(
            src_ref=src,
            dst_ref=dst,
            send_sem=halo_send.at[index],
            recv_sem=halo_recv.at[index],
            device_id=device,
            device_id_type=MESH,
        )

    def lat_halo(buf, base):
        up = halo_copy(
            buf.at[1, pl.ds(0, PAD)], buf.at[17, pl.ds(0, PAD)], base, {"lat": lax.max(lat - 1, 0)}
        )
        down = halo_copy(
            buf.at[16, pl.ds(0, PAD)],
            buf.at[0, pl.ds(0, PAD)],
            base + 1,
            {"lat": lax.min(lat + 1, ROWS - 1)},
        )
        return up, down

    def lon_halo(buf, end, base):
        pairs = []
        for n, rows in enumerate((pl.ds(1, ROWS), pl.ds(0, 1), pl.ds(17, 1))):
            pairs.append(
                (
                    halo_copy(
                        buf.at[rows, pl.ds(0, SPREAD)],
                        buf.at[rows, pl.ds(PAD, SPREAD)],
                        base + 2 + 2 * n,
                        {"lon": left},
                    ),
                    halo_copy(
                        end.at[rows],
                        buf.at[rows, pl.ds(PAD + SPREAD, SPREAD)],
                        base + 3 + 2 * n,
                        {"lon": right},
                    ),
                )
            )
        return pairs

    def tail_row(buf, end, i):
        moved = pltpu.roll(buf[i, 0:PAD, :].astype(F32), PAD - COLS, 0)
        end[i] = moved[PAD - SPREAD : PAD].astype(BF16)

    def halo_begin(buf, end, base):
        up, down = lat_halo(buf, base)

        @pl.when(lat > 0)
        def _():
            up.start()

        @pl.when(lat < ROWS - 1)
        def _():
            down.start()

        def body(i, carry):
            tail_row(buf, end, i + 1)
            return carry

        lax.fori_loop(0, ROWS, body, 0)
        for copy in lon_halo(buf, end, base)[0]:
            copy.start()

    def halo_middle(buf, end, base):
        up, down = lat_halo(buf, base)

        @pl.when(lat > 0)
        def _():
            down.wait_recv()

        @pl.when(lat == 0)
        def _():
            buf[0, 0:PAD, :] = jnp.zeros((PAD, CHANNELS), BF16)

        @pl.when(lat < ROWS - 1)
        def _():
            up.wait_recv()

        @pl.when(lat == ROWS - 1)
        def _():
            buf[17, 0:PAD, :] = jnp.zeros((PAD, CHANNELS), BF16)

        tail_row(buf, end, 0)
        tail_row(buf, end, 17)
        for pair in lon_halo(buf, end, base)[1:]:
            for copy in pair:
                copy.start()

    def halo_wait_main(buf, end, base):
        for copy in lon_halo(buf, end, base)[0]:
            copy.wait_recv()

    def halo_wait_edge(buf, end, base):
        for pair in lon_halo(buf, end, base)[1:]:
            for copy in pair:
                copy.wait_recv()

    def halo_end(buf, end, base):
        up, down = lat_halo(buf, base)

        @pl.when(lat > 0)
        def _():
            up.wait_send()

        @pl.when(lat < ROWS - 1)
        def _():
            down.wait_send()

        for pair in lon_halo(buf, end, base):
            for copy in pair:
                copy.wait_send()

    lane = lax.broadcasted_iota(jnp.int32, (PAD, WIDE), 1)
    row = lax.broadcasted_iota(jnp.int32, (PAD, WIDE), 0)
    direct = (row < COLS) & ((lane < COLS) | (lane >= PAD + SPREAD))
    shifted = (row < COLS) & (lane >= PAD) & (lane < PAD + SPREAD)

    def band_row(vecs, buf, i, backward):
        for k in range(3):
            for r in range(3):
                if backward:
                    vec = vecs[3 * k + 2 - r, pl.ds(i + r, 1), :]
                else:
                    vec = vecs[3 * k + r, pl.ds(i + 1, 1), :]
                near = pltpu.roll(jnp.broadcast_to(vec, (PAD, WIDE)), 0, 1, stride=1, stride_axis=0)
                far = pltpu.roll(
                    jnp.broadcast_to(vec, (32, WIDE)), 64 + PAD - COLS, 1, stride=1, stride_axis=0
                )
                high = jnp.where(direct[64:], near[64:], jnp.where(shifted[64:], far, 0.0))
                lanes = slice(r * WIDE, (r + 1) * WIDE)
                band[k * PAD : k * PAD + 64, lanes] = jnp.where(direct[:64], near[:64], 0.0).astype(
                    BF16
                )
                band[k * PAD + 64 : (k + 1) * PAD, lanes] = high.astype(BF16)
        around = buf[pl.ds(i, 3)].reshape(3 * WIDE, CHANNELS)
        value = jnp.dot(band[...], around, preferred_element_type=F32).astype(BF16)
        for k in range(3):
            resp[k, i] = value[k * PAD : (k + 1) * PAD]

    def inner_rows(vecs, buf, backward):
        def body(i, carry):
            band_row(vecs, buf, i, backward)
            return carry

        lax.fori_loop(1, ROWS - 1, body, 0)

    def edge_rows(vecs, buf, backward):
        def body(n, carry):
            band_row(vecs, buf, n * (ROWS - 1), backward)
            return carry

        lax.fori_loop(0, 2, body, 0)

    def tap_vectors():
        offsets = jnp.abs(lax.broadcasted_iota(jnp.int32, (33, 256), 0) - SPREAD)
        retained = offsets <= width_ref[...]
        first = lax.broadcasted_iota(jnp.int32, (32, 256), 0) + lat * ROWS - 1
        chosen = jnp.where(lax.broadcasted_iota(jnp.int32, (32, 256), 1) == first, 1.0, 0.0)
        tap = lax.broadcasted_iota(jnp.int32, (33, WIDE), 0)
        spot = lax.broadcasted_iota(jnp.int32, (33, WIDE), 1)
        ahead = jnp.where(((tap + WIDE - SPREAD) & (WIDE - 1)) == spot, 1.0, 0.0).astype(BF16)
        behind = jnp.where(((WIDE + SPREAD - tap) & (WIDE - 1)) == spot, 1.0, 0.0).astype(BF16)
        for k in range(3):
            for r in range(3):
                kept = jnp.where(retained, basis_ref[k, r].astype(F32), 0.0).astype(BF16)
                local = lax.dot_general(
                    chosen.astype(BF16), kept, (((1,), (1,)), ((), ())), preferred_element_type=F32
                ).astype(BF16)
                vf[3 * k + r] = jnp.dot(local, ahead, preferred_element_type=F32)
                vb[3 * k + r] = jnp.dot(local, behind, preferred_element_type=F32)

    def mix(transposed):
        def body(n, carry):
            total = jnp.zeros((TILE, CHANNELS), F32)
            for k in range(3):
                part = resp[k, pl.ds(4 * n, 4)].reshape(TILE, CHANNELS)
                total = total + lax.dot_general(
                    part,
                    mixv[k],
                    (((1,), (1 if transposed else 0,)), ((), ())),
                    preferred_element_type=F32,
                )
            dense[pl.ds(4 * n, 4)] = total.reshape(4, PAD, CHANNELS)
            return carry

        lax.fori_loop(0, 4, body, 0)

    def to_spectrum(table, field, h, target):
        def body(n, carry):
            rows = pl.ds(pl.multiple_of(n * TILE, TILE), TILE)
            target[rows, :] = jnp.dot(
                tables[table, rows, :],
                field[h].reshape(ROWS * PAD, LANES),
                preferred_element_type=F32,
            )
            return carry

        lax.fori_loop(0, 4, body, 0)

    def to_field(table, field, h):
        def body(n, carry):
            rows = pl.ds(pl.multiple_of(n * TILE, TILE), TILE)
            value = jnp.dot(tables[table, rows, :], modes[...], preferred_element_type=F32)
            field[h, pl.ds(4 * n, 4)] = value.astype(BF16).reshape(4, PAD, LANES)
            return carry

        lax.fori_loop(0, 4, body, 0)

    def chunk_start(source, target, stage, q, device):
        pltpu.make_async_remote_copy(
            src_ref=source,
            dst_ref=target,
            send_sem=ar_send.at[stage, q],
            recv_sem=ar_recv.at[stage, q],
            device_id=device,
            device_id_type=MESH,
        ).start()

    def pair_start(q):
        chunk_start(parts.at[q, 1 - core], pair_in.at[q], 0, q, {"lon": twin})

    def to_lat(source, target, stage, q):
        def body(step, carry):
            peer = lax.rem(lat + step, ROWS)
            chunk_start(source(peer), target, stage, q, {"lat": peer})
            return carry

        lax.fori_loop(1, ROWS, body, 0)

    def pair_finish(q):
        wait_bytes(pair_in.at[q], ar_recv.at[0, q])

        def body(n, carry):
            rows = pl.ds(6 * n, 6)
            both = parts[q, core, rows].astype(F32) + pair_in[q, rows].astype(F32)
            pair_sum[q, rows] = both.astype(BF16)
            return carry

        lax.fori_loop(0, 8, body, 0)
        to_lat(lambda peer: pair_sum.at[q, pl.ds(3 * peer, 3)], lat_in.at[q, lat], 1, q)
        lat_in[q, lat] = pair_sum[q, pl.ds(3 * lat, 3)]

    def lat_finish(q):
        wait_bytes(lat_in.at[q, pl.ds(0, ROWS - 1)], ar_recv.at[1, q])
        value = jnp.sum(lat_in[q].astype(F32), axis=0).astype(BF16)
        lat_sum[q] = value
        if q in SCATTERED:
            for t in range(3):
                owner = 3 * q + t

                @pl.when(chip == owner)
                def _():
                    z_tile[q, chip] = value[t]

                @pl.when(chip != owner)
                def _():
                    chunk_start(
                        lat_sum.at[q, t], z_tile.at[q, chip], 2, q, {"lon": 2 * owner + core}
                    )

            return
        z_in[q, chip] = value

        def body(step, carry):
            peer = lax.rem(me + 2 * step, ROWS)
            chunk_start(lat_sum.at[q], z_in.at[q, chip], 2, q, {"lon": peer})
            return carry

        lax.fori_loop(1, ROWS // 2, body, 0)

    def owns(q):
        return (chip >= 3 * q) & (chip < 3 * q + 3)

    def z_reduce(q):
        @pl.when(owns(q))
        def _():
            wait_bytes(z_tile.at[q, pl.ds(0, ROWS // 2 - 1)], ar_recv.at[2, q])
            slot = total.at[q, core, 3 * lat + chip - 3 * q]
            slot[...] = jnp.sum(z_tile[q].astype(F32), axis=0).astype(BF16)

            def body(step, carry):
                chunk_start(slot, slot, 5, q, {"lon": lax.rem(me + 2 * step, ROWS)})
                return carry

            lax.fori_loop(1, ROWS // 2, body, 0)

    def z_finish(q):
        mine = pl.ds(3 * lat, 3)
        if q in SCATTERED:

            @pl.when(owns(q))
            def _():
                wait_bytes(lat_sum.at[q, pl.ds(0, 2)], ar_recv.at[5, q])

            @pl.when(jnp.logical_not(owns(q)))
            def _():
                wait_bytes(lat_sum.at[q], ar_recv.at[5, q])

        else:
            wait_bytes(z_in.at[q, pl.ds(0, ROWS // 2 - 1)], ar_recv.at[2, q])
            total[q, core, mine] = jnp.sum(z_in[q].astype(F32), axis=0).astype(BF16)
        to_lat(lambda peer: total.at[q, core, mine], total.at[q, core, mine], 3, q)

    def gather_finish(q):
        wait_bytes(total.at[q, 0, pl.ds(0, 45)], ar_recv.at[3, q])
        chunk_start(total.at[q, core], total.at[q, core], 4, q, {"lon": twin})

    def chunk_wait(q):
        wait_bytes(total.at[q, 0], ar_recv.at[4, q])

    def chunk_end(q):
        wait_bytes(total.at[q, 0], ar_send.at[0, q])
        wait_bytes(total.at[q, 0, pl.ds(0, 45)], ar_send.at[1, q])
        if q in SCATTERED:

            @pl.when(owns(q))
            def _():
                wait_bytes(total.at[q, 0, pl.ds(0, 2)], ar_send.at[2, q])
                wait_bytes(total.at[q, 0, pl.ds(0, ROWS // 2 - 1)], ar_send.at[5, q])

            @pl.when(jnp.logical_not(owns(q)))
            def _():
                wait_bytes(total.at[q, 0, pl.ds(0, 3)], ar_send.at[2, q])

        else:
            wait_bytes(total.at[q, 0, pl.ds(0, 21)], ar_send.at[2, q])
        wait_bytes(total.at[q, 0, pl.ds(0, 45)], ar_send.at[3, q])
        wait_bytes(total.at[q, 0], ar_send.at[4, q])

    spread_start(xs, g1, 0, 0)
    halo_begin(slab, tail, 0)
    spread_start(xs, g1, 1, 0)
    for h in range(2):
        own_piece(xs, g1, h)
    tap_vectors()
    loads[0].wait()
    unfold(ctv, store_ct)
    modes[WAVES:WAVES_PAD, :] = jnp.zeros((WAVES_PAD - WAVES, LANES), BF16)
    modes[WAVES_PAD + WAVES :, :] = jnp.zeros((WAVES_PAD - WAVES, LANES), BF16)
    for h in range(2):
        for c in range(2):
            parts[1 + h, c, 45:48] = jnp.zeros((3, 16, LANES), BF16)
    halo_middle(slab, tail, 0)
    STEP = 144
    BATCH = 6
    LAST = 7
    for copy in loads[1:]:
        copy.wait()

    for h in range(2):
        lanes = slice(h * LANES, (h + 1) * LANES)
        spread_wait(g1, h, 0)
        to_spectrum(0, g1, h, spectrum.at[h])

        def gain(n, carry):
            low = pl.ds(pl.multiple_of(n * STEP, 16), STEP)
            high = pl.ds(pl.multiple_of(WAVES_PAD + n * STEP, 16), STEP)
            real_part, imag_part = spectrum[h, low, :], spectrum[h, high, :]
            real_gain, imag_gain = sfv[0, low, lanes], sfv[1, low, lanes]
            modes[low, :] = (real_gain * real_part - imag_gain * imag_part).astype(BF16)
            modes[high, :] = (real_gain * imag_part + imag_gain * real_part).astype(BF16)
            return carry

        lax.fori_loop(0, WAVES // STEP, gain, 0)
        to_field(1, ys, h)
        spread_start(ys, s1, h, 1)
        own_piece(ys, s1, h)
        if h == 0:
            halo_wait_main(slab, tail, 0)
            inner_rows(vf, slab, False)

    halo_wait_edge(slab, tail, 0)
    edge_rows(vf, slab, False)
    mix(False)

    for h in range(2):
        lanes = slice(h * LANES, (h + 1) * LANES)
        spread_wait(s1, h, 1)

        def activate(i, carry):
            preact = dense[i, :, lanes] + s1[h, i].astype(F32)
            logistic = 1.0 / (1.0 + jnp.exp(-preact))
            own = slab[i + 1, 0:PAD, lanes].astype(F32)
            outs[i, :, lanes] = (own + preact * logistic).astype(BF16)
            slope = logistic * (1.0 + preact * (1.0 - logistic))
            grad = (cts[i, :, lanes].astype(F32) * slope).astype(BF16)
            ps[h, i] = grad
            pslab[i + 1, 0:PAD, lanes] = grad
            return carry

        lax.fori_loop(0, ROWS, activate, 0)
        if h == 1:
            halo_begin(pslab, ptail, 8)
        spread_start(ps, g2, h, 2, 0, ROWS - 1 if h == 0 else BATCH)
        own_piece(ps, g2, h)

    for k in range(3):
        part = lax.dot_general(
            resp[k].reshape(ROWS * PAD, CHANNELS),
            pslab[1:17, 0:PAD, :].reshape(ROWS * PAD, CHANNELS),
            (((0,), (0,)), ((), ())),
            preferred_element_type=F32,
        ).astype(BF16)
        for c in range(2):
            parts[0, c, 16 * k : 16 * (k + 1)] = part[:, c * LANES : (c + 1) * LANES].reshape(
                16, 16, LANES
            )
    pair_start(0)
    halo_middle(pslab, ptail, 8)
    pair_finish(0)
    fold(outs, folded, slice(0, CHANNELS))
    out_store = pltpu.make_async_copy(folded, out_ref, store_sem.at[0])
    out_store.start()
    lat_finish(0)
    spread_start(ps, g2, 1, 2, BATCH, ROWS - 1)

    for h in range(2):
        lanes = slice(h * LANES, (h + 1) * LANES)
        spread_wait(g2, h, 2)
        if h == 1:
            z_finish(0)
        to_spectrum(2, g2, h, cotspec)

        def back(n, carry):
            low = pl.ds(pl.multiple_of(n * STEP, 16), STEP)
            high = pl.ds(pl.multiple_of(WAVES_PAD + n * STEP, 16), STEP)
            real_part, imag_part = spectrum[h, low, :], spectrum[h, high, :]
            real_cot, imag_cot = cotspec[low, :], cotspec[high, :]
            real_gain, imag_gain = sfv[0, low, lanes], sfv[1, low, lanes]
            modes[low, :] = (real_gain * real_cot + imag_gain * imag_cot).astype(BF16)
            modes[high, :] = (real_gain * imag_cot - imag_gain * real_cot).astype(BF16)
            first = real_cot * real_part + imag_cot * imag_part
            second = imag_cot * real_part - real_cot * imag_part
            parts[1 + h, 0, pl.ds(9 * n, 9)] = first.astype(BF16).reshape(9, 16, LANES)
            parts[1 + h, 1, pl.ds(9 * n, 9)] = second.astype(BF16).reshape(9, 16, LANES)
            return carry

        lax.fori_loop(0, WAVES // STEP, back, 0)
        pair_start(1 + h)
        if h == 1:
            pair_finish(2)
        to_field(3, zs, h)
        if h == 0:
            z_reduce(0)
            spread_start(zs, s2, h, 3, 0, BATCH)
            own_piece(zs, s2, h)
            pair_finish(1)
            halo_wait_main(pslab, ptail, 8)
            inner_rows(vb, pslab, True)
            lat_finish(1)
            spread_start(zs, s2, h, 3, BATCH, ROWS - 1)
        else:
            spread_start(zs, s2, h, 3, 0, LAST)
            own_piece(zs, s2, h)

    halo_wait_edge(pslab, ptail, 8)
    edge_rows(vb, pslab, True)
    lat_finish(2)
    spread_start(zs, s2, 1, 3, LAST, ROWS - 1)
    z_finish(1)
    gather_finish(0)
    mix(True)

    def finish(h):
        lanes = slice(h * LANES, (h + 1) * LANES)
        spread_wait(s2, h, 3)

        def body(i, carry):
            value = dense[i, :, lanes] + s2[h, i].astype(F32)
            outs[i, :, lanes] = (cts[i, :, lanes].astype(F32) + value).astype(BF16)
            return carry

        lax.fori_loop(0, ROWS, body, 0)
        fold(outs, gfold, lanes)
        store = pltpu.make_async_copy(
            gfold.at[:, :, lanes], gin_ref.at[:, :, lanes], store_sem.at[1 + h]
        )
        store.start()
        return store

    def chunk_out(q):
        chunk_wait(q)
        store = pltpu.make_async_copy(total.at[q], sum_ref.at[q], store_sem.at[3 + q])
        store.start()
        return store

    z_finish(2)
    finals = [chunk_out(0), finish(0)]
    gather_finish(1)
    finals.append(chunk_out(1))
    gather_finish(2)
    finals.append(finish(1))
    finals.append(chunk_out(2))

    for phase, source in enumerate((xs, ys, ps, zs)):
        for h in range(2):
            wait_bytes(source.at[h, pl.ds(0, ROWS - 1)], a_send.at[phase, h])
    halo_end(slab, tail, 0)
    halo_end(pslab, ptail, 8)
    for q in range(3):
        chunk_end(q)
    out_store.wait()
    for store in finals:
        store.wait()


def deliver(
    out_ref, gin_ref, sum_ref, out_to, gin_to, gw_to, gf_to, out, gin, sums, gw, gf, arrived, left
):
    loads = [pltpu.make_async_copy(sum_ref.at[q], sums.at[q], arrived.at[q]) for q in range(3)]
    loads.append(pltpu.make_async_copy(out_ref, out, arrived.at[3]))
    loads.append(pltpu.make_async_copy(gin_ref, gin, arrived.at[4]))
    stores = [
        pltpu.make_async_copy(source, target, left.at[i])
        for i, (source, target) in enumerate(
            ((gw, gw_to), (gf.at[0], gf_to.at[0]), (gf.at[1], gf_to.at[1]), (out, out_to), (gin, gin_to))
        )
    ]
    for copy in loads:
        copy.start()
    loads[0].wait()
    for k in range(3):
        for c in range(2):
            gw[k, :, c * LANES : (c + 1) * LANES] = (
                sums[0, c, 16 * k : 16 * (k + 1)].reshape(CHANNELS, LANES).astype(F32)
            )
    stores[0].start()
    loads[1].wait()
    loads[2].wait()
    for c in range(2):
        for h in range(2):
            gf[c, :, h * LANES : (h + 1) * LANES] = (
                sums[1 + h, c, 0:45].reshape(WAVES, LANES).astype(F32)
            )
        stores[1 + c].start()
    for i in (3, 4):
        loads[i].wait()
        stores[i].start()
    for copy in stores:
        copy.wait()


def on_device(features, cotangent, disco_basis, support_width, mix_weight, spectral_filter):
    tables = [jnp.asarray(t) for t in dft_tables()]
    vmem = pl.BlockSpec(memory_space=pltpu.VMEM)
    hbm = pl.BlockSpec(memory_space=pl.ANY)
    pieces = (2, ROWS, PAD, LANES)
    field = jax.ShapeDtypeStruct((COLS, ROWS, CHANNELS), BF16)
    sums = jax.ShapeDtypeStruct((3, 2, 48, 16, LANES), BF16)
    results = pl.pallas_call(
        kernel,
        out_shape=[field, field, sums],
        in_specs=[vmem, hbm, vmem, vmem] + [hbm] * 6,
        out_specs=[hbm, hbm, hbm],
        scratch_shapes=[
            pltpu.VMEM((4, ROWS * PAD, ROWS * PAD), BF16),
            pltpu.VMEM((COLS, ROWS, CHANNELS), BF16),
            pltpu.VMEM((3, CHANNELS, CHANNELS), BF16),
            pltpu.VMEM((2, WAVES, CHANNELS), F32),
            pltpu.VMEM((256, 256), BF16),
            pltpu.VMEM((9, 32, WIDE), F32),
            pltpu.VMEM((9, 32, WIDE), F32),
            pltpu.VMEM((ROWS, PAD, CHANNELS), BF16),
            pltpu.VMEM((ROWS + 2, WIDE, CHANNELS), BF16),
            pltpu.VMEM((ROWS + 2, WIDE, CHANNELS), BF16),
            pltpu.VMEM((ROWS + 2, SPREAD, CHANNELS), BF16),
            pltpu.VMEM((ROWS + 2, SPREAD, CHANNELS), BF16),
        ]
        + [pltpu.VMEM(pieces, BF16)] * 8
        + [
            pltpu.VMEM((3, ROWS, PAD, CHANNELS), BF16),
            pltpu.VMEM((ROWS, PAD, CHANNELS), F32),
            pltpu.VMEM((2, 2 * WAVES_PAD, LANES), F32),
            pltpu.VMEM((2 * WAVES_PAD, LANES), F32),
            pltpu.VMEM((2 * WAVES_PAD, LANES), BF16),
            pltpu.VMEM((3 * PAD, 3 * WIDE), BF16),
            pltpu.VMEM((ROWS, PAD, CHANNELS), BF16),
            pltpu.VMEM((COLS, ROWS, CHANNELS), BF16),
            pltpu.VMEM((COLS, ROWS, CHANNELS), BF16),
            pltpu.VMEM((3, 2, 48, 16, LANES), BF16),
            pltpu.VMEM((3, 48, 16, LANES), BF16),
            pltpu.VMEM((3, 48, 16, LANES), BF16),
            pltpu.VMEM((3, ROWS, 3, 16, LANES), BF16),
            pltpu.VMEM((3, 3, 16, LANES), BF16),
            pltpu.VMEM((3, ROWS // 2, 3, 16, LANES), BF16),
            pltpu.VMEM((3, ROWS // 2, 16, LANES), BF16),
            pltpu.VMEM((3, 2, 48, 16, LANES), BF16),
            pltpu.SemaphoreType.DMA((7,)),
            pltpu.SemaphoreType.DMA((6,)),
            pltpu.SemaphoreType.DMA((4, 2)),
            pltpu.SemaphoreType.DMA((4, 2)),
            pltpu.SemaphoreType.DMA((16,)),
            pltpu.SemaphoreType.DMA((16,)),
            pltpu.SemaphoreType.DMA((6, 3)),
            pltpu.SemaphoreType.DMA((6, 3)),
        ],
        compiler_params=pltpu.CompilerParams(
            collective_id=0, has_side_effects=True, vmem_limit_bytes=60 * 1024 * 1024
        ),
        cost_estimate=pl.CostEstimate(
            flops=8_000_000_000, bytes_accessed=30_000_000, transcendentals=400_000
        ),
    )(
        jnp.transpose(features, (1, 0, 2)),
        jnp.transpose(cotangent, (1, 0, 2)),
        jnp.transpose(disco_basis, (0, 2, 3, 1)),
        support_width.reshape(1, -1),
        mix_weight,
        spectral_filter,
        *tables,
    )
    shapes = [
        field,
        field,
        jax.ShapeDtypeStruct((3, CHANNELS, CHANNELS), F32),
        jax.ShapeDtypeStruct((2, WAVES, CHANNELS), F32),
    ]
    held = [field, field, sums] + shapes[2:]
    out, gin, gw, gf = pl.pallas_call(
        deliver,
        out_shape=shapes,
        in_specs=[hbm] * 3,
        out_specs=[hbm] * 4,
        scratch_shapes=[pltpu.VMEM(r.shape, r.dtype) for r in held]
        + [pltpu.SemaphoreType.DMA((5,)), pltpu.SemaphoreType.DMA((5,))],
        compiler_params=pltpu.CompilerParams(vmem_limit_bytes=60 * 1024 * 1024),
    )(*results)
    return (jnp.transpose(out, (1, 0, 2)), jnp.transpose(gin, (1, 0, 2)), gw, gf)


def solution(mesh):
    return jax.shard_map(
        on_device,
        mesh=mesh,
        in_specs=(P("lat", "lon", None), P("lat", "lon", None), P(), P(), P(), P()),
        out_specs=(P("lat", "lon", None), P("lat", "lon", None), P(), P()),
        check_vma=False,
    )
```

```python
import math

import jax
import jax.numpy as jnp
import ml_dtypes
import numpy as np
from jax import lax
from jax.experimental import pallas as pl
from jax.experimental.pallas import tpu as pltpu
from jax.sharding import PartitionSpec as P

MESH = pl.DeviceIdType.MESH
F32 = jnp.float32
BF16 = jnp.bfloat16

ROWS = 16
COLS = 90
PAD = 96
WAVES = 720
WAVES_PAD = 768
SPREAD = 16
LANES = 128
CHANNELS = 256
WIDE = 128
TILE = 384
SCATTERED = (0,)


def dft_tables():
    longitudes = ROWS * COLS
    cell_index = np.arange(longitudes, dtype=np.int64)
    wave_index = np.arange(WAVES, dtype=np.int64)
    phase_index = wave_index[:, None] * cell_index[None, :] % longitudes
    angles = phase_index.astype(np.float32) * np.float32(2.0 * math.pi / longitudes)
    cosine_wave = np.cos(angles)
    sine_wave = np.sin(angles)
    factor = np.where(wave_index == 0, 1.0, 2.0).astype(np.float32) / np.float32(longitudes)

    def padded(real, imag):
        table = np.zeros((2, WAVES_PAD, ROWS, PAD), np.float32)
        table[0, :WAVES, :, :COLS] = real.reshape(WAVES, ROWS, COLS)
        table[1, :WAVES, :, :COLS] = imag.reshape(WAVES, ROWS, COLS)
        return table.reshape(2 * WAVES_PAD, ROWS * PAD).astype(ml_dtypes.bfloat16)

    forward = padded(cosine_wave, -sine_wave)
    inverse_t = padded(cosine_wave * factor[:, None], -sine_wave * factor[:, None])
    return (
        forward,
        np.ascontiguousarray(inverse_t.T),
        inverse_t,
        np.ascontiguousarray(forward.T),
    )


def kernel(
    x_ref, ct_ref, basis_ref, width_ref, mix_ref, sf_ref, t0_ref, t1_ref, t2_ref, t3_ref,
    out_ref, gin_ref, sum_ref,
    tables, ctv, mixv, sfv, perm, vf, vb, cts, slab, pslab, tail, ptail,
    xs, g1, ys, s1, ps, g2, zs, s2,
    resp, dense, spectrum, cotspec, modes, band, outs, folded, gfold,
    parts, pair_in, pair_sum, lat_in, lat_sum, z_in, z_tile, total,
    load_sem, store_sem, a_send, a_recv, halo_send, halo_recv, ar_send, ar_recv,
):
    me = lax.axis_index("lon")
    lat = lax.axis_index("lat")
    right = lax.rem(me + 1, ROWS)
    left = lax.rem(me + ROWS - 1, ROWS)
    core = lax.rem(me, 2)
    chip = lax.div(me, 2)
    twin = me + 1 - 2 * core

    loads = [
        pltpu.make_async_copy(ref, target, load_sem.at[i])
        for i, (ref, target) in enumerate(
            (
                (ct_ref, ctv),
                (t0_ref, tables.at[0]),
                (sf_ref, sfv),
                (t1_ref, tables.at[1]),
                (mix_ref, mixv),
                (t2_ref, tables.at[2]),
                (t3_ref, tables.at[3]),
            )
        )
    ]
    for copy in loads:
        copy.start()

    barrier = pltpu.get_barrier_semaphore()

    def greet(step, carry):
        pl.semaphore_signal(
            barrier, inc=1, device_id={"lon": lax.rem(me + step, ROWS)}, device_id_type=MESH
        )
        pl.semaphore_signal(
            barrier, inc=1, device_id={"lat": lax.rem(lat + step, ROWS)}, device_id_type=MESH
        )
        return carry

    lax.fori_loop(1, ROWS, greet, 0)

    a = lax.broadcasted_iota(jnp.int32, (256, 256), 0)
    b = lax.broadcasted_iota(jnp.int32, (256, 256), 1)
    perm[...] = jnp.where(b == (a & 15) * 16 + (a >> 4), 1.0, 0.0).astype(BF16)

    def unfold(source, store):
        for g in range(6):
            count = min(16, COLS - 16 * g)
            data = source[16 * g : 16 * g + count].reshape(count * ROWS, CHANNELS)
            value = jnp.dot(perm[:, 0 : count * ROWS], data, preferred_element_type=F32)
            store(slice(16 * g, 16 * g + 16), value.astype(BF16).reshape(ROWS, 16, CHANNELS))

    def fold(source, target, lanes):
        for g in range(6):
            count = min(16, COLS - 16 * g)
            data = source[:, 16 * g : 16 * g + 16, lanes]
            width = data.shape[2]
            value = jnp.dot(perm[...], data.reshape(256, width), preferred_element_type=F32)
            value = value.astype(BF16).reshape(16, ROWS, width)
            target[16 * g : 16 * g + count, :, lanes] = value[0:count]

    def store_x(columns, value):
        slab[1:17, columns, :] = value
        for h in range(2):
            xs[h, :, columns, :] = value[:, :, h * LANES : (h + 1) * LANES]

    def store_ct(columns, value):
        cts[:, columns, :] = value

    unfold(x_ref, store_x)
    pl.semaphore_wait(barrier, 2 * (ROWS - 1))

    def offset(step):
        return 8 + (1 - 2 * lax.rem(step, 2)) * lax.div(step + 1, 2)

    def spread_start(source, target, h, phase, first=0, end=ROWS - 1):
        def body(step, carry):
            peer = lax.rem(me + offset(step), ROWS)
            pltpu.make_async_remote_copy(
                src_ref=source.at[h, peer],
                dst_ref=target.at[h, me],
                send_sem=a_send.at[phase, h],
                recv_sem=a_recv.at[phase, h],
                device_id={"lon": peer},
                device_id_type=MESH,
            ).start()
            return carry

        lax.fori_loop(first, end, body, 0)

    def own_piece(source, target, h):
        target[h, me] = source[h, me]

    def wait_bytes(ref, sem):
        pltpu.make_async_copy(ref, ref, sem).wait()

    def spread_wait(target, h, phase):
        wait_bytes(target.at[h, pl.ds(0, ROWS - 1)], a_recv.at[phase, h])

    def halo_copy(src, dst, index, device):
        return pltpu.make_async_remote_copy(
            src_ref=src,
            dst_ref=dst,
            send_sem=halo_send.at[index],
            recv_sem=halo_recv.at[index],
            device_id=device,
            device_id_type=MESH,
        )

    def lat_halo(buf, base):
        up = halo_copy(
            buf.at[1, pl.ds(0, PAD)], buf.at[17, pl.ds(0, PAD)], base, {"lat": lax.max(lat - 1, 0)}
        )
        down = halo_copy(
            buf.at[16, pl.ds(0, PAD)],
            buf.at[0, pl.ds(0, PAD)],
            base + 1,
            {"lat": lax.min(lat + 1, ROWS - 1)},
        )
        return up, down

    def lon_halo(buf, end, base):
        pairs = []
        for n, rows in enumerate((pl.ds(1, ROWS), pl.ds(0, 1), pl.ds(17, 1))):
            pairs.append(
                (
                    halo_copy(
                        buf.at[rows, pl.ds(0, SPREAD)],
                        buf.at[rows, pl.ds(PAD, SPREAD)],
                        base + 2 + 2 * n,
                        {"lon": left},
                    ),
                    halo_copy(
                        end.at[rows],
                        buf.at[rows, pl.ds(PAD + SPREAD, SPREAD)],
                        base + 3 + 2 * n,
                        {"lon": right},
                    ),
                )
            )
        return pairs

    def tail_row(buf, end, i):
        moved = pltpu.roll(buf[i, 0:PAD, :].astype(F32), PAD - COLS, 0)
        end[i] = moved[PAD - SPREAD : PAD].astype(BF16)

    def halo_begin(buf, end, base):
        up, down = lat_halo(buf, base)

        @pl.when(lat > 0)
        def _():
            up.start()

        @pl.when(lat < ROWS - 1)
        def _():
            down.start()

        def body(i, carry):
            tail_row(buf, end, i + 1)
            return carry

        lax.fori_loop(0, ROWS, body, 0)
        for copy in lon_halo(buf, end, base)[0]:
            copy.start()

    def halo_middle(buf, end, base):
        up, down = lat_halo(buf, base)

        @pl.when(lat > 0)
        def _():
            down.wait_recv()

        @pl.when(lat == 0)
        def _():
            buf[0, 0:PAD, :] = jnp.zeros((PAD, CHANNELS), BF16)

        @pl.when(lat < ROWS - 1)
        def _():
            up.wait_recv()

        @pl.when(lat == ROWS - 1)
        def _():
            buf[17, 0:PAD, :] = jnp.zeros((PAD, CHANNELS), BF16)

        tail_row(buf, end, 0)
        tail_row(buf, end, 17)
        for pair in lon_halo(buf, end, base)[1:]:
            for copy in pair:
                copy.start()

    def halo_wait_main(buf, end, base):
        for copy in lon_halo(buf, end, base)[0]:
            copy.wait_recv()

    def halo_wait_edge(buf, end, base):
        for pair in lon_halo(buf, end, base)[1:]:
            for copy in pair:
                copy.wait_recv()

    def halo_end(buf, end, base):
        up, down = lat_halo(buf, base)

        @pl.when(lat > 0)
        def _():
            up.wait_send()

        @pl.when(lat < ROWS - 1)
        def _():
            down.wait_send()

        for pair in lon_halo(buf, end, base):
            for copy in pair:
                copy.wait_send()

    lane = lax.broadcasted_iota(jnp.int32, (PAD, WIDE), 1)
    row = lax.broadcasted_iota(jnp.int32, (PAD, WIDE), 0)
    direct = (row < COLS) & ((lane < COLS) | (lane >= PAD + SPREAD))
    shifted = (row < COLS) & (lane >= PAD) & (lane < PAD + SPREAD)

    def band_row(vecs, buf, i, backward):
        for k in range(3):
            for r in range(3):
                if backward:
                    vec = vecs[3 * k + 2 - r, pl.ds(i + r, 1), :]
                else:
                    vec = vecs[3 * k + r, pl.ds(i + 1, 1), :]
                near = pltpu.roll(jnp.broadcast_to(vec, (PAD, WIDE)), 0, 1, stride=1, stride_axis=0)
                far = pltpu.roll(
                    jnp.broadcast_to(vec, (32, WIDE)), 64 + PAD - COLS, 1, stride=1, stride_axis=0
                )
                high = jnp.where(direct[64:], near[64:], jnp.where(shifted[64:], far, 0.0))
                lanes = slice(r * WIDE, (r + 1) * WIDE)
                band[k * PAD : k * PAD + 64, lanes] = jnp.where(direct[:64], near[:64], 0.0).astype(
                    BF16
                )
                band[k * PAD + 64 : (k + 1) * PAD, lanes] = high.astype(BF16)
        around = buf[pl.ds(i, 3)].reshape(3 * WIDE, CHANNELS)
        value = jnp.dot(band[...], around, preferred_element_type=F32).astype(BF16)
        for k in range(3):
            resp[k, i] = value[k * PAD : (k + 1) * PAD]

    def inner_rows(vecs, buf, backward):
        def body(i, carry):
            band_row(vecs, buf, i, backward)
            return carry

        lax.fori_loop(1, ROWS - 1, body, 0)

    def edge_rows(vecs, buf, backward):
        def body(n, carry):
            band_row(vecs, buf, n * (ROWS - 1), backward)
            return carry

        lax.fori_loop(0, 2, body, 0)

    def tap_vectors():
        offsets = jnp.abs(lax.broadcasted_iota(jnp.int32, (33, 256), 0) - SPREAD)
        retained = offsets <= width_ref[...]
        first = lax.broadcasted_iota(jnp.int32, (32, 256), 0) + lat * ROWS - 1
        chosen = jnp.where(lax.broadcasted_iota(jnp.int32, (32, 256), 1) == first, 1.0, 0.0)
        tap = lax.broadcasted_iota(jnp.int32, (33, WIDE), 0)
        spot = lax.broadcasted_iota(jnp.int32, (33, WIDE), 1)
        ahead = jnp.where(((tap + WIDE - SPREAD) & (WIDE - 1)) == spot, 1.0, 0.0).astype(BF16)
        behind = jnp.where(((WIDE + SPREAD - tap) & (WIDE - 1)) == spot, 1.0, 0.0).astype(BF16)
        for k in range(3):
            for r in range(3):
                kept = jnp.where(retained, basis_ref[k, r].astype(F32), 0.0).astype(BF16)
                local = lax.dot_general(
                    chosen.astype(BF16), kept, (((1,), (1,)), ((), ())), preferred_element_type=F32
                ).astype(BF16)
                vf[3 * k + r] = jnp.dot(local, ahead, preferred_element_type=F32)
                vb[3 * k + r] = jnp.dot(local, behind, preferred_element_type=F32)

    def mix(transposed):
        def body(n, carry):
            total = jnp.zeros((TILE, CHANNELS), F32)
            for k in range(3):
                part = resp[k, pl.ds(4 * n, 4)].reshape(TILE, CHANNELS)
                total = total + lax.dot_general(
                    part,
                    mixv[k],
                    (((1,), (1 if transposed else 0,)), ((), ())),
                    preferred_element_type=F32,
                )
            dense[pl.ds(4 * n, 4)] = total.reshape(4, PAD, CHANNELS)
            return carry

        lax.fori_loop(0, 4, body, 0)

    def to_spectrum(table, field, h, target):
        def body(n, carry):
            rows = pl.ds(pl.multiple_of(n * TILE, TILE), TILE)
            target[rows, :] = jnp.dot(
                tables[table, rows, :],
                field[h].reshape(ROWS * PAD, LANES),
                preferred_element_type=F32,
            )
            return carry

        lax.fori_loop(0, 4, body, 0)

    def to_field(table, field, h):
        def body(n, carry):
            rows = pl.ds(pl.multiple_of(n * TILE, TILE), TILE)
            value = jnp.dot(tables[table, rows, :], modes[...], preferred_element_type=F32)
            field[h, pl.ds(4 * n, 4)] = value.astype(BF16).reshape(4, PAD, LANES)
            return carry

        lax.fori_loop(0, 4, body, 0)

    def chunk_start(source, target, stage, q, device):
        pltpu.make_async_remote_copy(
            src_ref=source,
            dst_ref=target,
            send_sem=ar_send.at[stage, q],
            recv_sem=ar_recv.at[stage, q],
            device_id=device,
            device_id_type=MESH,
        ).start()

    def pair_start(q):
        chunk_start(parts.at[q, 1 - core], pair_in.at[q], 0, q, {"lon": twin})

    def to_lat(source, target, stage, q):
        def body(step, carry):
            peer = lax.rem(lat + step, ROWS)
            chunk_start(source(peer), target, stage, q, {"lat": peer})
            return carry

        lax.fori_loop(1, ROWS, body, 0)

    def pair_finish(q):
        wait_bytes(pair_in.at[q], ar_recv.at[0, q])

        def body(n, carry):
            rows = pl.ds(6 * n, 6)
            both = parts[q, core, rows].astype(F32) + pair_in[q, rows].astype(F32)
            pair_sum[q, rows] = both.astype(BF16)
            return carry

        lax.fori_loop(0, 8, body, 0)
        to_lat(lambda peer: pair_sum.at[q, pl.ds(3 * peer, 3)], lat_in.at[q, lat], 1, q)
        lat_in[q, lat] = pair_sum[q, pl.ds(3 * lat, 3)]

    def lat_finish(q):
        wait_bytes(lat_in.at[q, pl.ds(0, ROWS - 1)], ar_recv.at[1, q])
        value = jnp.sum(lat_in[q].astype(F32), axis=0).astype(BF16)
        lat_sum[q] = value
        if q in SCATTERED:
            for t in range(3):
                owner = 3 * q + t

                @pl.when(chip == owner)
                def _():
                    z_tile[q, chip] = value[t]

                @pl.when(chip != owner)
                def _():
                    chunk_start(
                        lat_sum.at[q, t], z_tile.at[q, chip], 2, q, {"lon": 2 * owner + core}
                    )

            return
        z_in[q, chip] = value

        def body(step, carry):
            peer = lax.rem(me + 2 * step, ROWS)
            chunk_start(lat_sum.at[q], z_in.at[q, chip], 2, q, {"lon": peer})
            return carry

        lax.fori_loop(1, ROWS // 2, body, 0)

    def owns(q):
        return (chip >= 3 * q) & (chip < 3 * q + 3)

    def z_reduce(q):
        @pl.when(owns(q))
        def _():
            wait_bytes(z_tile.at[q, pl.ds(0, ROWS // 2 - 1)], ar_recv.at[2, q])
            slot = total.at[q, core, 3 * lat + chip - 3 * q]
            slot[...] = jnp.sum(z_tile[q].astype(F32), axis=0).astype(BF16)

            def body(step, carry):
                chunk_start(slot, slot, 5, q, {"lon": lax.rem(me + 2 * step, ROWS)})
                return carry

            lax.fori_loop(1, ROWS // 2, body, 0)

    def z_finish(q):
        mine = pl.ds(3 * lat, 3)
        if q in SCATTERED:

            @pl.when(owns(q))
            def _():
                wait_bytes(lat_sum.at[q, pl.ds(0, 2)], ar_recv.at[5, q])

            @pl.when(jnp.logical_not(owns(q)))
            def _():
                wait_bytes(lat_sum.at[q], ar_recv.at[5, q])

        else:
            wait_bytes(z_in.at[q, pl.ds(0, ROWS // 2 - 1)], ar_recv.at[2, q])
            total[q, core, mine] = jnp.sum(z_in[q].astype(F32), axis=0).astype(BF16)
        to_lat(lambda peer: total.at[q, core, mine], total.at[q, core, mine], 3, q)

    def gather_finish(q):
        wait_bytes(total.at[q, 0, pl.ds(0, 45)], ar_recv.at[3, q])
        chunk_start(total.at[q, core], total.at[q, core], 4, q, {"lon": twin})

    def chunk_wait(q):
        wait_bytes(total.at[q, 0], ar_recv.at[4, q])

    def chunk_end(q):
        wait_bytes(total.at[q, 0], ar_send.at[0, q])
        wait_bytes(total.at[q, 0, pl.ds(0, 45)], ar_send.at[1, q])
        if q in SCATTERED:

            @pl.when(owns(q))
            def _():
                wait_bytes(total.at[q, 0, pl.ds(0, 2)], ar_send.at[2, q])
                wait_bytes(total.at[q, 0, pl.ds(0, ROWS // 2 - 1)], ar_send.at[5, q])

            @pl.when(jnp.logical_not(owns(q)))
            def _():
                wait_bytes(total.at[q, 0, pl.ds(0, 3)], ar_send.at[2, q])

        else:
            wait_bytes(total.at[q, 0, pl.ds(0, 21)], ar_send.at[2, q])
        wait_bytes(total.at[q, 0, pl.ds(0, 45)], ar_send.at[3, q])
        wait_bytes(total.at[q, 0], ar_send.at[4, q])

    spread_start(xs, g1, 0, 0)
    halo_begin(slab, tail, 0)
    spread_start(xs, g1, 1, 0)
    for h in range(2):
        own_piece(xs, g1, h)
    tap_vectors()
    loads[0].wait()
    unfold(ctv, store_ct)
    modes[WAVES:WAVES_PAD, :] = jnp.zeros((WAVES_PAD - WAVES, LANES), BF16)
    modes[WAVES_PAD + WAVES :, :] = jnp.zeros((WAVES_PAD - WAVES, LANES), BF16)
    for h in range(2):
        for c in range(2):
            parts[1 + h, c, 45:48] = jnp.zeros((3, 16, LANES), BF16)
    halo_middle(slab, tail, 0)
    STEP = 144
    BATCH = 6
    LAST = 7
    for copy in loads[1:]:
        copy.wait()

    for h in range(2):
        lanes = slice(h * LANES, (h + 1) * LANES)
        spread_wait(g1, h, 0)
        to_spectrum(0, g1, h, spectrum.at[h])

        def gain(n, carry):
            low = pl.ds(pl.multiple_of(n * STEP, 16), STEP)
            high = pl.ds(pl.multiple_of(WAVES_PAD + n * STEP, 16), STEP)
            real_part, imag_part = spectrum[h, low, :], spectrum[h, high, :]
            real_gain, imag_gain = sfv[0, low, lanes], sfv[1, low, lanes]
            modes[low, :] = (real_gain * real_part - imag_gain * imag_part).astype(BF16)
            modes[high, :] = (real_gain * imag_part + imag_gain * real_part).astype(BF16)
            return carry

        lax.fori_loop(0, WAVES // STEP, gain, 0)
        to_field(1, ys, h)
        spread_start(ys, s1, h, 1)
        own_piece(ys, s1, h)
        if h == 0:
            halo_wait_main(slab, tail, 0)
            inner_rows(vf, slab, False)

    halo_wait_edge(slab, tail, 0)
    edge_rows(vf, slab, False)
    mix(False)

    for h in range(2):
        lanes = slice(h * LANES, (h + 1) * LANES)
        spread_wait(s1, h, 1)

        def activate(i, carry):
            preact = dense[i, :, lanes] + s1[h, i].astype(F32)
            logistic = 1.0 / (1.0 + jnp.exp(-preact))
            own = slab[i + 1, 0:PAD, lanes].astype(F32)
            outs[i, :, lanes] = (own + preact * logistic).astype(BF16)
            slope = logistic * (1.0 + preact * (1.0 - logistic))
            grad = (cts[i, :, lanes].astype(F32) * slope).astype(BF16)
            ps[h, i] = grad
            pslab[i + 1, 0:PAD, lanes] = grad
            return carry

        lax.fori_loop(0, ROWS, activate, 0)
        if h == 1:
            halo_begin(pslab, ptail, 8)
        spread_start(ps, g2, h, 2, 0, ROWS - 1 if h == 0 else BATCH)
        own_piece(ps, g2, h)

    for k in range(3):
        part = lax.dot_general(
            resp[k].reshape(ROWS * PAD, CHANNELS),
            pslab[1:17, 0:PAD, :].reshape(ROWS * PAD, CHANNELS),
            (((0,), (0,)), ((), ())),
            preferred_element_type=F32,
        ).astype(BF16)
        for c in range(2):
            parts[0, c, 16 * k : 16 * (k + 1)] = part[:, c * LANES : (c + 1) * LANES].reshape(
                16, 16, LANES
            )
    pair_start(0)
    halo_middle(pslab, ptail, 8)
    pair_finish(0)
    fold(outs, folded, slice(0, CHANNELS))
    out_store = pltpu.make_async_copy(folded, out_ref, store_sem.at[0])
    out_store.start()
    lat_finish(0)
    spread_start(ps, g2, 1, 2, BATCH, ROWS - 1)

    for h in range(2):
        lanes = slice(h * LANES, (h + 1) * LANES)
        spread_wait(g2, h, 2)
        if h == 1:
            z_finish(0)
        to_spectrum(2, g2, h, cotspec)

        def back(n, carry):
            low = pl.ds(pl.multiple_of(n * STEP, 16), STEP)
            high = pl.ds(pl.multiple_of(WAVES_PAD + n * STEP, 16), STEP)
            real_part, imag_part = spectrum[h, low, :], spectrum[h, high, :]
            real_cot, imag_cot = cotspec[low, :], cotspec[high, :]
            real_gain, imag_gain = sfv[0, low, lanes], sfv[1, low, lanes]
            modes[low, :] = (real_gain * real_cot + imag_gain * imag_cot).astype(BF16)
            modes[high, :] = (real_gain * imag_cot - imag_gain * real_cot).astype(BF16)
            first = real_cot * real_part + imag_cot * imag_part
            second = imag_cot * real_part - real_cot * imag_part
            parts[1 + h, 0, pl.ds(9 * n, 9)] = first.astype(BF16).reshape(9, 16, LANES)
            parts[1 + h, 1, pl.ds(9 * n, 9)] = second.astype(BF16).reshape(9, 16, LANES)
            return carry

        lax.fori_loop(0, WAVES // STEP, back, 0)
        pair_start(1 + h)
        if h == 1:
            pair_finish(2)
        to_field(3, zs, h)
        if h == 0:
            z_reduce(0)
            spread_start(zs, s2, h, 3, 0, BATCH)
            own_piece(zs, s2, h)
            pair_finish(1)
            halo_wait_main(pslab, ptail, 8)
            inner_rows(vb, pslab, True)
            lat_finish(1)
            spread_start(zs, s2, h, 3, BATCH, ROWS - 1)
        else:
            spread_start(zs, s2, h, 3, 0, LAST)
            own_piece(zs, s2, h)

    halo_wait_edge(pslab, ptail, 8)
    edge_rows(vb, pslab, True)
    lat_finish(2)
    spread_start(zs, s2, 1, 3, LAST, ROWS - 1)
    z_finish(1)
    gather_finish(0)
    mix(True)

    def finish(h):
        lanes = slice(h * LANES, (h + 1) * LANES)
        spread_wait(s2, h, 3)

        def body(i, carry):
            value = dense[i, :, lanes] + s2[h, i].astype(F32)
            outs[i, :, lanes] = (cts[i, :, lanes].astype(F32) + value).astype(BF16)
            return carry

        lax.fori_loop(0, ROWS, body, 0)
        fold(outs, gfold, lanes)
        store = pltpu.make_async_copy(
            gfold.at[:, :, lanes], gin_ref.at[:, :, lanes], store_sem.at[1 + h]
        )
        store.start()
        return store

    def chunk_out(q):
        chunk_wait(q)
        store = pltpu.make_async_copy(total.at[q], sum_ref.at[q], store_sem.at[3 + q])
        store.start()
        return store

    z_finish(2)
    finals = [chunk_out(0), finish(0)]
    gather_finish(1)
    finals.append(chunk_out(1))
    gather_finish(2)
    finals.append(finish(1))
    finals.append(chunk_out(2))

    for phase, source in enumerate((xs, ys, ps, zs)):
        for h in range(2):
            wait_bytes(source.at[h, pl.ds(0, ROWS - 1)], a_send.at[phase, h])
    halo_end(slab, tail, 0)
    halo_end(pslab, ptail, 8)
    for q in range(3):
        chunk_end(q)
    out_store.wait()
    for store in finals:
        store.wait()


def deliver(
    out_ref, gin_ref, sum_ref, out_to, gin_to, gw_to, gf_to, out, gin, sums, gw, gf, arrived, left
):
    loads = [pltpu.make_async_copy(sum_ref.at[q], sums.at[q], arrived.at[q]) for q in range(3)]
    loads.append(pltpu.make_async_copy(out_ref, out, arrived.at[3]))
    loads.append(pltpu.make_async_copy(gin_ref, gin, arrived.at[4]))
    stores = [
        pltpu.make_async_copy(source, target, left.at[i])
        for i, (source, target) in enumerate(
            ((gw, gw_to), (gf.at[0], gf_to.at[0]), (gf.at[1], gf_to.at[1]), (out, out_to), (gin, gin_to))
        )
    ]
    for i in (3, 4, 0, 1, 2):
        loads[i].start()
    for i in (3, 4):
        loads[i].wait()
        stores[i].start()
    loads[0].wait()
    for k in range(3):
        for c in range(2):
            gw[k, :, c * LANES : (c + 1) * LANES] = (
                sums[0, c, 16 * k : 16 * (k + 1)].reshape(CHANNELS, LANES).astype(F32)
            )
    stores[0].start()
    loads[1].wait()
    loads[2].wait()
    for c in range(2):
        for h in range(2):
            gf[c, :, h * LANES : (h + 1) * LANES] = (
                sums[1 + h, c, 0:45].reshape(WAVES, LANES).astype(F32)
            )
        stores[1 + c].start()
    for copy in stores:
        copy.wait()


def on_device(features, cotangent, disco_basis, support_width, mix_weight, spectral_filter):
    tables = [jnp.asarray(t) for t in dft_tables()]
    vmem = pl.BlockSpec(memory_space=pltpu.VMEM)
    hbm = pl.BlockSpec(memory_space=pl.ANY)
    pieces = (2, ROWS, PAD, LANES)
    field = jax.ShapeDtypeStruct((COLS, ROWS, CHANNELS), BF16)
    sums = jax.ShapeDtypeStruct((3, 2, 48, 16, LANES), BF16)
    results = pl.pallas_call(
        kernel,
        out_shape=[field, field, sums],
        in_specs=[vmem, hbm, vmem, vmem] + [hbm] * 6,
        out_specs=[hbm, hbm, hbm],
        scratch_shapes=[
            pltpu.VMEM((4, ROWS * PAD, ROWS * PAD), BF16),
            pltpu.VMEM((COLS, ROWS, CHANNELS), BF16),
            pltpu.VMEM((3, CHANNELS, CHANNELS), BF16),
            pltpu.VMEM((2, WAVES, CHANNELS), F32),
            pltpu.VMEM((256, 256), BF16),
            pltpu.VMEM((9, 32, WIDE), F32),
            pltpu.VMEM((9, 32, WIDE), F32),
            pltpu.VMEM((ROWS, PAD, CHANNELS), BF16),
            pltpu.VMEM((ROWS + 2, WIDE, CHANNELS), BF16),
            pltpu.VMEM((ROWS + 2, WIDE, CHANNELS), BF16),
            pltpu.VMEM((ROWS + 2, SPREAD, CHANNELS), BF16),
            pltpu.VMEM((ROWS + 2, SPREAD, CHANNELS), BF16),
        ]
        + [pltpu.VMEM(pieces, BF16)] * 8
        + [
            pltpu.VMEM((3, ROWS, PAD, CHANNELS), BF16),
            pltpu.VMEM((ROWS, PAD, CHANNELS), F32),
            pltpu.VMEM((2, 2 * WAVES_PAD, LANES), F32),
            pltpu.VMEM((2 * WAVES_PAD, LANES), F32),
            pltpu.VMEM((2 * WAVES_PAD, LANES), BF16),
            pltpu.VMEM((3 * PAD, 3 * WIDE), BF16),
            pltpu.VMEM((ROWS, PAD, CHANNELS), BF16),
            pltpu.VMEM((COLS, ROWS, CHANNELS), BF16),
            pltpu.VMEM((COLS, ROWS, CHANNELS), BF16),
            pltpu.VMEM((3, 2, 48, 16, LANES), BF16),
            pltpu.VMEM((3, 48, 16, LANES), BF16),
            pltpu.VMEM((3, 48, 16, LANES), BF16),
            pltpu.VMEM((3, ROWS, 3, 16, LANES), BF16),
            pltpu.VMEM((3, 3, 16, LANES), BF16),
            pltpu.VMEM((3, ROWS // 2, 3, 16, LANES), BF16),
            pltpu.VMEM((3, ROWS // 2, 16, LANES), BF16),
            pltpu.VMEM((3, 2, 48, 16, LANES), BF16),
            pltpu.SemaphoreType.DMA((7,)),
            pltpu.SemaphoreType.DMA((6,)),
            pltpu.SemaphoreType.DMA((4, 2)),
            pltpu.SemaphoreType.DMA((4, 2)),
            pltpu.SemaphoreType.DMA((16,)),
            pltpu.SemaphoreType.DMA((16,)),
            pltpu.SemaphoreType.DMA((6, 3)),
            pltpu.SemaphoreType.DMA((6, 3)),
        ],
        compiler_params=pltpu.CompilerParams(
            collective_id=0, has_side_effects=True, vmem_limit_bytes=60 * 1024 * 1024
        ),
        cost_estimate=pl.CostEstimate(
            flops=8_000_000_000, bytes_accessed=30_000_000, transcendentals=400_000
        ),
    )(
        jnp.transpose(features, (1, 0, 2)),
        jnp.transpose(cotangent, (1, 0, 2)),
        jnp.transpose(disco_basis, (0, 2, 3, 1)),
        support_width.reshape(1, -1),
        mix_weight,
        spectral_filter,
        *tables,
    )
    shapes = [
        field,
        field,
        jax.ShapeDtypeStruct((3, CHANNELS, CHANNELS), F32),
        jax.ShapeDtypeStruct((2, WAVES, CHANNELS), F32),
    ]
    held = [field, field, sums] + shapes[2:]
    out, gin, gw, gf = pl.pallas_call(
        deliver,
        out_shape=shapes,
        in_specs=[hbm] * 3,
        out_specs=[hbm] * 4,
        scratch_shapes=[pltpu.VMEM(r.shape, r.dtype) for r in held]
        + [pltpu.SemaphoreType.DMA((5,)), pltpu.SemaphoreType.DMA((5,))],
        compiler_params=pltpu.CompilerParams(vmem_limit_bytes=60 * 1024 * 1024),
    )(*results)
    return (jnp.transpose(out, (1, 0, 2)), jnp.transpose(gin, (1, 0, 2)), gw, gf)


def solution(mesh):
    return jax.shard_map(
        on_device,
        mesh=mesh,
        in_specs=(P("lat", "lon", None), P("lat", "lon", None), P(), P(), P(), P()),
        out_specs=(P("lat", "lon", None), P("lat", "lon", None), P(), P()),
        check_vma=False,
    )
```
